128 devices in a mesh: space: 32 (over y, z, x_hi), tm: 4 (over x_lo, core).
Axes of the slice: x: 4 (x_hi: 2, x_lo: 2; x = x_hi * 2 + x_lo), y: 4, z: 4, core: 2. Of those that a mesh axis runs over, the one named last changes fastest.
Arguments:
- pw_field: float32 [96, 128, 36864], P('space', 'tm'), may hold values from -6 to 6
- cell_area: float32 [16, 36864], replicated, may hold values from 0.5 to 1.5
- tile_ids: int32 [96], replicated, may hold values from 0 to 95, as said below
- edge_table: int32 [3, 96, 4], replicated, may hold values from 0 to 95, as said below
Outputs:
- gram: float32 [128, 128], P('tm')
The draws below stay inside these ranges and needn't reach their ends.
Inputs may be any that keep to these rules, and one draw needn't show every extreme that they name: A permutation: slot s holds the tile of face tile_ids[s] // 16, row (tile_ids[s] // 4) mod 4, column tile_ids[s] mod 4 of the face. `edge_table`: the cube's gluing for the slots of tile_ids: the neighbour slot and edge across each edge, and 1 where the two edges run in opposite directions; flags and edges lie in 0 to 1 and 0 to 3.
All inputs are finite; a program needn't handle non-finite values.
Results may differ from the reference program's by a relative error of at most 0.000051.
Values sent between devices are 32-bit elements; how exact they have to be, the bound alone decides.
No kernel may reach another device: no remote copies, remote signals or barrier semaphores. Data moves between devices by JAX's collectives and lax.ppermute only.
A program may use at most 704 MiB of HBM per device.

```python
import math
import jax
import jax.numpy as jnp
from jax import lax

SUB = 4
STRIDE = 4
STEPS = 4
TILE = 192
TILES = 96
SNAPS = 128


FRAMES = [((1, 0, 0), (0, 1, 0), (0, 0, 1)), ((0, 1, 0), (-1, 0, 0), (0, 0, 1)), ((-1, 0, 0), (0, -1, 0), (0, 0, 1)), ((0, -1, 0), (1, 0, 0), (0, 0, 1)), ((0, 0, 1), (0, 1, 0), (-1, 0, 0)), ((0, 0, -1), (0, 1, 0), (1, 0, 0))]


def corner_key(center, axis_u, axis_v, coord_a, coord_b, sub_count):
    return tuple((sub_count * center[index_c] + coord_a * axis_u[index_c] + coord_b * axis_v[index_c] for index_c in range(3)))


def cube_table(sub_count):
    tiles_total = 6 * sub_count * sub_count
    records = {}
    for face_idx in range(6):
        center, axis_u, axis_v = FRAMES[face_idx]
        for row_tile in range(sub_count):
            for col_tile in range(sub_count):
                tile_idx = face_idx * sub_count * sub_count + row_tile * sub_count + col_tile
                low_a = -sub_count + 2 * row_tile
                high_a = low_a + 2
                low_b = -sub_count + 2 * col_tile
                high_b = low_b + 2
                edge_ends = [((low_a, low_b), (low_a, high_b)), ((high_a, low_b), (high_a, high_b)), ((low_a, low_b), (high_a, low_b)), ((low_a, high_b), (high_a, high_b))]
                for edge_idx in range(4):
                    end_keys = []
                    for coord_a, coord_b in edge_ends[edge_idx]:
                        end_keys.append(corner_key(center, axis_u, axis_v, coord_a, coord_b, sub_count))
                    joint_key = tuple(sorted(end_keys))
                    entry = (tile_idx, edge_idx, end_keys[0])
                    if joint_key in records:
                        records[joint_key].append(entry)
                    else:
                        records[joint_key] = [entry]
    near_tile = [[0] * 4 for _ in range(tiles_total)]
    near_edge = [[0] * 4 for _ in range(tiles_total)]
    near_flip = [[0] * 4 for _ in range(tiles_total)]
    for paired in records.values():
        for own_end, far_end in ((paired[0], paired[1]), (paired[1], paired[0])):
            near_tile[own_end[0]][own_end[1]] = far_end[0]
            near_edge[own_end[0]][own_end[1]] = far_end[1]
            near_flip[own_end[0]][own_end[1]] = 0 if own_end[2] == far_end[2] else 1
    return (near_tile, near_edge, near_flip)


def slot_layout(key):
    order = jax.random.permutation(key, TILES).astype(jnp.int32)
    near_tile, near_edge, near_flip = cube_table(SUB)
    tile_table = jnp.asarray(near_tile, dtype=jnp.int32)
    edge_list = jnp.asarray(near_edge, dtype=jnp.int32)
    flip_list = jnp.asarray(near_flip, dtype=jnp.int32)
    slot_of = jnp.zeros((TILES,), jnp.int32).at[order].set(jnp.arange(TILES, dtype=jnp.int32))
    near_slot = slot_of[tile_table[order]]
    table = jnp.stack([near_slot, edge_list[order], flip_list[order]])
    return (order, table.astype(jnp.int32))


def draw_tile_ids(key, part):
    layout = slot_layout(key)
    key = jax.random.fold_in(key, 1)
    return layout[0]


def draw_edge_table(key, part):
    layout = slot_layout(key)
    key = jax.random.fold_in(key, 2)
    return layout[1]


def draw_pw_field(key, part):
    key = jax.random.fold_in(key, 3)
    sub_keys = jax.random.split(key, 4)
    full_shape = (TILES, SNAPS, TILE * TILE)
    rough_part = jax.random.normal(sub_keys[0], full_shape, jnp.float32)
    return jnp.clip(rough_part, -6.0, 6.0)


def setup_inputs(seed: int = 0) -> dict:
    key_list = jax.random.split(jax.random.key(seed), 5)
    pw_field = draw_pw_field(jax.random.fold_in(key_list[4], 71), 0)
    cell_area = jnp.clip(jnp.exp(jax.random.uniform(key_list[1], (SUB * SUB, TILE * TILE), jnp.float32, math.log(0.5), math.log(1.5))), 0.5, 1.5)
    tile_ids = draw_tile_ids(jax.random.fold_in(key_list[4], 71), 0)
    edge_table = draw_edge_table(jax.random.fold_in(key_list[4], 71), 0)
    return {"pw_field": pw_field, "cell_area": cell_area, "tile_ids": tile_ids, "edge_table": edge_table}


def coefficient(step_idx):
    return 0.12 + 0.1 * step_idx / max(STEPS - 1, 1)


def edge_strips(weighted):
    return jnp.stack([weighted[:, :, :TILE], weighted[:, :, -TILE:], weighted[:, :, 0::TILE], weighted[:, :, TILE - 1::TILE]], axis=1)


def pick_halo(all_strips, near_slot, near_edge, near_flip):
    snap_count = all_strips.shape[2]
    edge_width = all_strips.shape[3]
    flat_strips = all_strips.reshape(-1, snap_count, edge_width)
    position = (near_slot * 4 + near_edge).reshape(-1)
    chosen = jnp.take(flat_strips, position, axis=0).reshape(near_slot.shape[0], 4, snap_count, edge_width)
    return jnp.where((near_flip == 1)[:, :, None, None], chosen[..., ::-1], chosen)


def smooth_step(values, weighted, tile_area, halo_rows, factor):
    column = jnp.arange(TILE * TILE, dtype=jnp.int32) % TILE
    upper_nb = jnp.concatenate([halo_rows[:, 0], weighted[:, :, :-TILE]], axis=2)
    lower_nb = jnp.concatenate([weighted[:, :, TILE:], halo_rows[:, 1]], axis=2)
    left_shift = jnp.concatenate([weighted[:, :, :1], weighted[:, :, :-1]], axis=2)
    right_shift = jnp.concatenate([weighted[:, :, 1:], weighted[:, :, -1:]], axis=2)
    left_nb = jnp.where(column == 0, jnp.repeat(halo_rows[:, 2], TILE, axis=2), left_shift)
    right_nb = jnp.where(column == TILE - 1, jnp.repeat(halo_rows[:, 3], TILE, axis=2), right_shift)
    return values + factor * (upper_nb + lower_nb + left_nb + right_nb - 4.0 * weighted) / tile_area[:, None]


def subsample(values):
    shaped = values.reshape(values.shape[0], values.shape[1], TILE, TILE)[:, :, 1::STRIDE, 1::STRIDE]
    return shaped.reshape(values.shape[0], values.shape[1], -1)


def reference(pw_field, cell_area, tile_ids, edge_table):
    tile_area = jnp.take(cell_area, tile_ids % cell_area.shape[0], axis=0)

    def one_snapshot(snap_index):
        values = lax.dynamic_slice_in_dim(pw_field, snap_index, 1, 1)
        for step_idx in range(STEPS):
            weighted = tile_area[:, None] * values
            halo_rows = pick_halo(edge_strips(weighted), edge_table[0], edge_table[1], edge_table[2])
            values = smooth_step(values, weighted, tile_area, halo_rows, coefficient(step_idx))
        return subsample(values)[:, 0]

    sampled = lax.map(one_snapshot, jnp.arange(SNAPS, dtype=jnp.int32))
    snap_rows = sampled.reshape(SNAPS, -1)
    weights = subsample(tile_area[:, None])[:, 0].reshape(-1)
    full_gram = jnp.dot(snap_rows * weights, snap_rows.T, precision=lax.Precision.HIGHEST, preferred_element_type=jnp.float32)
    return full_gram / snap_rows.shape[1]
```

```python
import functools

import jax
import jax.numpy as jnp
import ml_dtypes
import numpy as np
from jax import lax
from jax.experimental import pallas as pl
from jax.experimental.pallas import tpu as pltpu
from jax.sharding import Mesh
from jax.sharding import PartitionSpec as P

STRIDE = 4
STEPS = 4
TILE = 192
CELLS = TILE * TILE
SAMP = TILE // STRIDE
AXES = ("y", "z", "xh", "xl", "c")
PAD = 640
SB = 16
F32 = jnp.float32
BF16 = jnp.bfloat16


def stencil():
    k = np.zeros((9, 9))
    k[4, 4] = 1.0
    for step in range(STEPS):
        c = 0.12 + 0.1 * step / max(STEPS - 1, 1)
        p = np.pad(k, 1)
        lap = p[:-2, 1:-1] + p[2:, 1:-1] + p[1:-1, :-2] + p[1:-1, 2:] - 4 * k
        k = k + c * lap
    return k[4:, 4:]


K = stencil()


def coef(d, m):
    return float(K[d, m]) if d + m <= STEPS else 0.0


CORNER = coef(2, 2) / 2.0
NEAR = {1: 0, 0: 1, 2: 1, 3: 2}
FAR = {1: 4, 0: 3, 2: 3, 3: 9}


def lane_tables():
    lane = np.arange(128) % 4
    near = np.array([[coef(d, NEAR[l]) for l in lane] for d in range(5)])
    far = np.array([[coef(d, FAR[l]) for l in lane] for d in range(2)])
    return np.concatenate([near, far, np.zeros((1, 128))]).astype(np.float32)


def edge_coef(high, flip, depth, pos):
    m = NEAR[(pos % 4) if not flip else ((3 - pos) % 4)]
    return coef(depth + 2 + high, m)


def row_edge_table():
    out = np.zeros((16, 128))
    for high in range(2):
        for flip in range(2):
            for depth in range(3):
                for lane in range(128):
                    out[(2 * high + flip) * 4 + depth, lane] = edge_coef(high, flip, depth, lane)
    return out.astype(np.float32)


def col_lanes():
    where = {}
    for k in range(8):
        for par in range(2):
            for depth in range(3):
                where[((0 if par == 0 else 64) + depth + 6 * k) % 128] = (2 * k + par, 2, depth)
                where[((63 if par == 0 else 127) - depth + 6 * k) % 128] = (2 * k + par, 3, depth)
    return where


def col_edge_table():
    out = np.zeros((8, 128))
    for lane, (row, edge, depth) in col_lanes().items():
        for high in range(2):
            for flip in range(2):
                out[(edge - 2) * 4 + 2 * high + flip, lane] = edge_coef(high, flip, depth, row)
    return out.astype(np.float32)


def place(lanes, pos, j, value=1.0):
    lanes[pos, j] = value


def sum_matrix():
    s = np.zeros((384, SAMP))
    for c in range(TILE):
        for j in range(SAMP):
            d = abs(c - (4 * j + 1))
            if 3 <= d <= 4:
                s[c, j] = 1.0
            if d <= 2:
                s[192 + c, j] = 1.0
    return s


def quad_matrices():
    s = sum_matrix()
    a = np.zeros((4, 384, 256))
    b = np.zeros((4, 384, 256))
    for q in range(4):
        a[q, :, 48 * q : 48 * q + 48] = s
        a[q, :, 192 + q] = s[:, 0]
        a[q, :, 196 + q] = s[:, SAMP - 1]
        b[q, :, 64 + 48 * q : 64 + 48 * q + 48] = s
        b[q, :, q] = s[:, 0]
        b[q, :, 4 + q] = s[:, SAMP - 1]
    both = np.stack([a.reshape(1536, 256), b.reshape(1536, 256)])
    return both.astype(ml_dtypes.bfloat16)


def row_edge_matrix():
    m = np.zeros((256, 128))
    for pos in range(TILE):
        for j in range(SAMP):
            if abs(pos - (4 * j + 1)) <= 2:
                m[pos, j] = 1.0
            if abs((TILE - 1 - pos) - (4 * j + 1)) <= 2:
                m[pos, 64 + j] = 1.0
    for k in range(2):
        m[192 + k, 48 + k] = 1.0
        m[192 + k, 112 + k] = 1.0
    return m.astype(ml_dtypes.bfloat16)


def col_edge_matrix():
    m = np.zeros((12, 128, 256))
    for group in range(12):
        for lane, (row, edge, _) in col_lanes().items():
            pos = 16 * group + row
            for j in range(SAMP):
                if abs(pos - (4 * j + 1)) <= 2:
                    m[group, lane, (edge - 2) * 128 + j] = 1.0
                if abs((TILE - 1 - pos) - (4 * j + 1)) <= 2:
                    m[group, lane, (edge - 2) * 128 + 64 + j] = 1.0
    return m.reshape(1536, 256).astype(ml_dtypes.bfloat16)


def inner_mask():
    m = np.zeros((8, 384))
    for g in range(6):
        for lane in range(384):
            r, j = 8 * g + lane // 48, lane % 48
            m[g, lane] = float(0 < r < SAMP - 1 and 0 < j < SAMP - 1)
    return m.astype(np.float32)


def halves(v):
    hi = v.astype(BF16)
    return hi, (v - hi.astype(F32)).astype(BF16)


def lanes_of(shape):
    return lax.broadcasted_iota(jnp.int32, shape, len(shape) - 1)


def space_index():
    return lax.axis_index("y") * 8 + lax.axis_index("z") * 2 + lax.axis_index("xh")


def swap_ends(v, lane):
    return jnp.where(
        lane == 0,
        pltpu.roll(v, 128 - (SAMP - 1), 1),
        jnp.where(lane == SAMP - 1, pltpu.roll(v, SAMP - 1, 1), v),
    )


def filter_kernel(
    ids, table, x_ref, area_ref, quad_ref, rowm_ref, colm_ref, lane_ref, rowk_ref, colk_ref, mask_ref,
    keep_ref, send_ref, edge_ref,
    wp, lhs, lhs_area, root, packed, lrow, lcol, strip,
):
    tile, half = pl.program_id(0), pl.program_id(1)
    slot = 3 * space_index() + tile
    aid = ids[slot] % 16
    xl = lax.axis_index("xl")
    lane = lanes_of((SB, 128))
    row0 = pl.multiple_of(tile * 32 + half * SB, SB)

    @pl.when((tile == 0) & (half == 0))
    def _():
        wp[:, :PAD] = jnp.zeros((SB, PAD), F32)
        wp[:, PAD + CELLS :] = jnp.zeros((SB, 512), F32)
        strip[:, 96:, :] = jnp.zeros((8, 32, 128), F32)

    area8 = pl.multiple_of((aid // 8) * 8, 8)
    turn = (8 - aid % 8) % 8

    def area_row(off, size):
        return pltpu.roll(area_ref[pl.ds(area8, 8), pl.ds(off, size)], turn, 0)[0:1]

    def variant(edge):
        at = slot * 4 + edge
        return (table[1, at] & 1) * 2 + table[2, at]

    k2 = colk_ref[pl.ds(variant(2), 1), :] + colk_ref[pl.ds(4 + variant(3), 1), :]

    def weigh(g, _):
        start = pl.multiple_of(g * 3072, 128)
        acc = None
        for k in range(8):
            vs = []
            for part in range(3):
                off = pl.multiple_of(start + (3 * k + part) * 128, 128)
                w = x_ref[0, :, pl.ds(off, 128)] * area_row(off, 128)
                wp[:, pl.ds(pl.multiple_of(off + PAD, 128), 128)] = w
                vs.append(w)
            both = jnp.where(lane < 3, vs[0], jnp.where(lane >= 125, vs[2], vs[1]))
            if k == 0:
                acc = both
            else:
                moved = pltpu.roll(both, 6 * k, 1)
                mine = ((lane >= 6 * k - 3) & (lane < 6 * k + 3)) | ((lane >= 61 + 6 * k) & (lane < 67 + 6 * k))
                acc = jnp.where(mine, moved, acc)
        hi, lo = halves(acc * k2)
        at = pl.multiple_of(g * 128, 128)
        lcol[pl.ds(row0, SB), pl.ds(at, 128)] = hi
        lcol[pl.ds(pl.multiple_of(96 + row0, SB), SB), pl.ds(at, 128)] = lo
        return 0

    lax.fori_loop(0, 12, weigh, 0)

    near = [lane_ref[d : d + 1, :] for d in range(5)]
    far = [lane_ref[5 + d : 6 + d, :] for d in range(2)]
    wide = lambda k: jnp.concatenate([k, k], axis=1)
    near = [wide(k) for k in near]
    far = [wide(k) for k in far]

    def rows(g, _):
        for h in range(8):
            base = pl.multiple_of(g * 6144 + 768 * h + PAD, 128)

            def win(off):
                return wp[:, pl.ds(pl.multiple_of(base + off, 128), 256)]

            s0 = win(128)
            s1 = win(384) + win(0)
            s2 = win(512) + win(-256)
            s3 = win(768) + win(-384)
            s4 = win(896) + win(-640)
            va = near[0] * s0 + near[2] * s2 + near[4] * s4
            vb = near[1] * s1 + near[3] * s3
            v1 = va + pltpu.roll(vb, 64, 1)
            v2 = far[1] * s1 + pltpu.roll(far[0] * s0, 192, 1)
            parts = [v2[:, :128], jnp.where(lane < 64, v2[:, 128:], v1[:, :128]), v1[:, 128:]]
            for p, v in enumerate(parts):
                hi, lo = halves(v)
                at = (h % 4) * 384 + p * 128
                lhs[h // 4, pl.ds(pl.multiple_of(g * SB, SB), SB), at : at + 128] = hi
                lhs[h // 4, pl.ds(pl.multiple_of(96 + g * SB, SB), SB), at : at + 128] = lo
        return 0

    lax.fori_loop(0, 6, rows, 0)

    @pl.when(half == 0)
    def _():
        lane2 = lanes_of((1, 256))
        picked = (lane2 >= 64) & (lane2 % 4 == 1)
        for r in range(SAMP):
            g, h = r // 8, r % 8
            a = area_row(768 * r + 128, 256)
            lhs_area[h // 4, g : g + 1, (h % 4) * 384 : (h % 4) * 384 + 128] = jnp.zeros((1, 128), F32)
            lhs_area[h // 4, g : g + 1, (h % 4) * 384 + 128 : (h % 4) * 384 + 384] = jnp.where(picked, a, 0.0)
        outs = []
        for n in range(2):
            lhs_area[n, 6:16, :] = jnp.zeros((10, 1536), F32)
            v = lhs_area[n]
            hi = v.astype(BF16)
            rest = v - hi.astype(F32)
            mid = rest.astype(BF16)
            low = (rest - mid.astype(F32)).astype(BF16)
            o = jnp.dot(jnp.concatenate([hi, mid, low], axis=0), quad_ref[n], preferred_element_type=F32)
            outs.append(o[0:8] + o[16:24] + o[32:40])
        a, b = outs
        lane8 = lanes_of((8, 128))
        area = jnp.concatenate([a[:, :128], jnp.where(lane8 < 64, a[:, 128:], b[:, :128]), b[:, 128:]], axis=1)
        inner = mask_ref[...] > 0.0
        root[...] = jnp.where(inner, lax.rsqrt(jnp.where(inner, area, 1.0)), 0.0)

    out_a = jnp.dot(lhs[0], quad_ref[0], preferred_element_type=F32)
    out_b = jnp.dot(lhs[1], quad_ref[1], preferred_element_type=F32)
    out_a = out_a[:96] + out_a[96:]
    out_b = out_b[:96] + out_b[96:]
    left = jnp.zeros((SB, 128), F32)
    right = jnp.zeros((SB, 128), F32)
    for g in range(6):
        a, b = out_a[SB * g : SB * g + SB], out_b[SB * g : SB * g + SB]
        a1, b0 = a[:, 128:], b[:, :128]
        packed[g, :, 0:128] = a[:, :128] * root[g : g + 1, 0:128]
        packed[g, :, 128:256] = jnp.where(lane < 64, a1, b0) * root[g : g + 1, 128:256]
        packed[g, :, 256:384] = b[:, 128:] * root[g : g + 1, 256:384]
        at_a = (lane >= 8 * g) & (lane < 8 * g + 4)
        at_b = (lane >= 8 * g + 4) & (lane < 8 * g + 8)
        left = jnp.where(at_a, pltpu.roll(a1, (8 * g + 64) % 128, 1), left)
        left = jnp.where(at_b, pltpu.roll(b0, (8 * g + 4) % 128, 1), left)
        right = jnp.where(at_a, pltpu.roll(a1, (8 * g + 60) % 128, 1), right)
        right = jnp.where(at_b, b0 if g == 0 else pltpu.roll(b0, 8 * g, 1), right)
    keep_ref[...] = packed[pl.ds(3 * xl, 3)]
    send_ref[...] = packed[pl.ds(3 * (1 - xl), 3)]
    here = pl.ds(row0, SB)
    strip[4, here, :] = out_a[:SB, :128]
    strip[5, here, :] = swap_ends(pltpu.roll(out_b[80:96, 128:], 48, 1), lane)
    strip[6, here, :] = left
    strip[7, here, :] = swap_ends(right, lane)

    lane2 = lanes_of((SB, 256))

    def win(off):
        return wp[:, PAD + off : PAD + off + 256]

    for edge in range(2):
        if edge == 0:
            lines = [win(0), pltpu.roll(win(128), 192, 1), win(384)]
        else:
            lines = [pltpu.roll(win(36608), 192, 1), win(36480), pltpu.roll(win(36224), 192, 1)]
        v = variant(edge) * 4
        u = jnp.zeros((SB, 256), F32)
        for d in range(3):
            u = u + wide(rowk_ref[pl.ds(v + d, 1), :]) * lines[d]
        u0 = u[:, :128]
        first, second = lines[0][:, :128], lines[0][:, 128:]
        u1 = jnp.where(
            lane == 64,
            pltpu.roll(first, 64, 1) * CORNER,
            jnp.where(lane == 65, pltpu.roll(second, 2, 1) * CORNER, u[:, 128:]),
        )
        for p, v in enumerate((u0, u1)):
            hi, lo = halves(v)
            lrow[pl.ds(pl.multiple_of(edge * 96 + row0, SB), SB), 128 * p : 128 * p + 128] = hi
            lrow[pl.ds(pl.multiple_of(192 + edge * 96 + row0, SB), SB), 128 * p : 128 * p + 128] = lo

    @pl.when((tile == 2) & (half == 1))
    def _():
        cr = jnp.dot(lrow[...], rowm_ref[...], preferred_element_type=F32)
        cc = jnp.dot(lcol[...], colm_ref[...], preferred_element_type=F32)
        cr = cr[:192] + cr[192:]
        cc = cc[:96] + cc[96:]
        given = [cr[:96], cr[96:], cc[:, :128], cc[:, 128:]]
        lane32 = lanes_of((32, 128))
        for edge in range(4):
            for t in range(3):
                at = (3 * space_index() + t) * 4 + edge
                v = given[edge][32 * t : 32 * t + 32]
                v = jnp.where(table[2, at] == 1, pltpu.roll(v, 64, 1), v)
                strip[edge, 32 * t : 32 * t + 32, :] = jnp.where(table[1, at] & 1 == 1, swap_ends(v, lane32), v)
        turned = []
        for q in range(8):
            tr = jnp.transpose(strip[q])
            edge_ref[pl.ds(q, SAMP, stride=16), :] = tr[:SAMP]
            edge_ref[pl.ds(8 + q, SAMP, stride=16), :] = tr[:SAMP]
            if q < 2:
                turned.append([tr[48:49], tr[49:50]])
        lane1 = lanes_of((1, 128))
        for c in range(2):
            edge_ref[8 * c + 6 : 8 * c + 7, :] = turned[0][0]
            edge_ref[8 * c + 7 : 8 * c + 8, :] = turned[0][1]
            for end in range(2):
                for t in range(3):
                    at = 8 * c + 3 * end + t
                    moved = pltpu.roll(turned[1][end], 96 - 32 * t, 1)
                    edge_ref[at : at + 1, :] = jnp.where(lane1 >= 96, moved, edge_ref[at : at + 1, :])


def gram_kernel(
    ids, table, got_ref, keep_ref, recv_ref, keep2_ref, recv2_ref, area_ref, out_ref,
    z, h, w, areas, hl, full,
):
    xl, c = lax.axis_index("xl"), lax.axis_index("c")
    chip = space_index() * 2 + xl
    first, last = chip == 0, chip == SAMP - 1
    lane = lanes_of((8, 128))
    sub = lax.broadcasted_iota(jnp.int32, (8, 128), 0)

    for ref, row in (
        (keep_ref, 2 * xl + c),
        (recv_ref, 2 * (1 - xl) + c),
        (keep2_ref, 2 * xl + 1 - c),
        (recv2_ref, 2 * (1 - xl) + 1 - c),
    ):
        at = pl.multiple_of(row * 32, 32)
        for b in range(9):
            hi, lo = halves(ref[b])
            hl[pl.ds(at, 32), 384 * b : 384 * b + 384] = hi
            hl[pl.ds(pl.multiple_of(128 + at, 32), 32), 384 * b : 384 * b + 384] = lo

    @pl.when(chip >= SAMP)
    def _():
        hl[:, 3456:] = jnp.zeros((256, 384), BF16)

    @pl.when(chip < SAMP)
    def _():
        def spread(s, _):
            v = [got_ref[pl.ds(pl.multiple_of(s * 32 + 8 * t, 8), 8), :] for t in range(4)]
            for i in range(4):
                acc = v[i]
                for t in range(4):
                    if t != i:
                        acc = jnp.where(lane // 32 == t, pltpu.roll(v[t], (32 * (t - i)) % 128, 1), acc)
                if i < 3:
                    z[pl.ds(pl.multiple_of(s * 24 + 8 * i, 8), 8), :] = acc
                else:
                    z[pl.ds(pl.multiple_of(768 + s * 8, 8), 8), :] = acc
            return 0

        lax.fori_loop(0, 32, spread, 0, unroll=2)

        cell = 4 * chip + 1
        swap = jnp.where(first, 4 * (SAMP - 1) + 1, jnp.where(last, 1, cell))
        spots = (192 + cell, 189 * 192 + swap, cell * 192 + 1, cell * 192 + 189)
        lane16 = lanes_of((16, 128))
        for e, spot in enumerate(spots):
            a = area_ref[:, pl.ds(pl.multiple_of((spot // 128) * 128, 128), 128)]
            a = jnp.sum(jnp.where(lane16 == spot % 128, a, 0.0), axis=1, keepdims=True)
            v = jnp.broadcast_to(lax.rsqrt(a), (16, 128))
            if e >= 2:
                v = jnp.where(first | last, 0.0, v)
            areas[pl.ds(4 + e, 16, stride=8), :] = v

        @pl.when(first)
        def _():
            def corner(slot, _):
                total = z[pl.ds(slot * 8 + 4, 1), :]
                for edge in (0, 2):
                    at = slot * 4 + edge
                    n1, e1, f1 = table[0, at], table[1, at], table[2, at]
                    side = n1 * 4 + 2 * (1 - (e1 >> 1)) + f1
                    n2, e2, f2 = table[0, side], table[1, side], table[2, side]
                    b2 = (e1 & 1) ^ f2
                    row = jnp.where(e2 < 2, e2, b2)
                    col = jnp.where(e2 < 2, b2, e2 - 2)
                    s2 = n2 // 3
                    spare = 768 + s2 * 8 + 3 * col + (n2 - 3 * s2)
                    where = jnp.where(row == 0, n2 * 8 + 6 + col, spare)
                    total = total + z[pl.ds(where, 1), :]
                h[pl.ds(slot, 1), :] = total
                return 0

            lax.fori_loop(0, 96, corner, 0)

            def put(slot, _):
                z[pl.ds(slot * 8 + 4, 1), :] = h[pl.ds(slot, 1), :]
                return 0

            lax.fori_loop(0, 96, put, 0)

        def gather(slot, _):
            for e in range(4):
                at = slot * 4 + e
                h[pl.ds(slot * 8 + 4 + e, 1), :] = z[pl.ds(table[0, at] * 8 + table[1, at], 1), :]
            return 0

        lax.fori_loop(0, 96, gather, 0, unroll=4)
        fx = jnp.where(first, 1.0, 0.0)
        fy = jnp.where(last, 1.0, 0.0)

        def total(pair, _):
            both = []
            for n in range(2):
                slot = pair * 2 + n
                at = pl.ds(pl.multiple_of(slot * 8, 8), 8)
                hv = jnp.where(sub >= 4, h[at, :], 0.0)
                extra = fx * pltpu.roll(hv, 6, 0) + fy * jnp.where(sub == 4, pltpu.roll(hv, 5, 0), pltpu.roll(hv, 7, 0))
                v = z[at, :] + hv + jnp.where(sub < 6, extra, 0.0)
                both.append(v * areas[pl.ds(pl.multiple_of((ids[slot] % 16) * 8, 8), 8), :])
            w[pl.ds(pl.multiple_of(pair * 8, 8), 8), :] = jnp.where(sub < 4, pltpu.roll(both[0], 4, 0), both[1])
            return 0

        lax.fori_loop(0, 48, total, 0, unroll=2)
        for p in range(3):
            hi, lo = halves(jnp.transpose(w[128 * p : 128 * p + 128, :]))
            at = 3456 + 128 * p
            hl[:128, at : at + 128] = hi
            hl[128:, at : at + 128] = lo

    g = lax.dot_general(hl[:128], hl[...], (((1,), (1,)), ((), ())), preferred_element_type=F32)
    cross = g[:, 128:]
    full[...] = g[:, :128] + cross + jnp.transpose(cross)
    for k in range(2):
        block = full[pl.ds(pl.multiple_of(64 * k + 32 * c, 32), 32), :]
        out_ref[k] = block
        out_ref[2 + k] = block


def body(pw_field, cell_area, tile_ids, edge_table):
    table = edge_table.reshape(3, 384)
    consts = [
        quad_matrices(), row_edge_matrix(), col_edge_matrix(), lane_tables(), row_edge_table(), col_edge_table(), inner_mask(),
    ]
    consts = [jnp.asarray(v) for v in consts]
    whole = lambda v: pl.BlockSpec(v.shape, functools.partial(lambda n, *_: (0,) * n, v.ndim), pipeline_mode=pl.Buffered(1))
    part = pl.BlockSpec((3, SB, 384), lambda i, h, *_: (i, h, 0))
    keep, send, edges = pl.pallas_call(
        filter_kernel,
        grid_spec=pltpu.PrefetchScalarGridSpec(
            num_scalar_prefetch=2,
            grid=(3, 2),
            in_specs=[pl.BlockSpec((1, SB, CELLS), lambda i, h, *_: (i, h, 0)), whole(cell_area)] + [whole(v) for v in consts],
            out_specs=[part, part, pl.BlockSpec((1024, 128), lambda i, h, *_: (0, 0))],
            scratch_shapes=[
                pltpu.VMEM((SB, PAD + CELLS + 512), F32),
                pltpu.VMEM((2, 192, 1536), BF16),
                pltpu.VMEM((2, 16, 1536), F32),
                pltpu.VMEM((8, 384), F32),
                pltpu.VMEM((6, SB, 384), F32),
                pltpu.VMEM((384, 256), BF16),
                pltpu.VMEM((192, 1536), BF16),
                pltpu.VMEM((8, 128, 128), F32),
            ],
        ),
        out_shape=[
            jax.ShapeDtypeStruct((9, 32, 384), F32),
            jax.ShapeDtypeStruct((9, 32, 384), F32),
            jax.ShapeDtypeStruct((1024, 128), F32),
        ],
        compiler_params=pltpu.CompilerParams(dimension_semantics=("arbitrary", "arbitrary"), vmem_limit_bytes=48 * 2**20),
        name="filter",
    )(tile_ids, table, pw_field, cell_area, *consts)

    flip = [(0, 1), (1, 0)]
    recv = lax.ppermute(send, "xl", flip)
    keep2 = lax.ppermute(keep, "c", flip)
    got = lax.all_to_all(edges.reshape(128, 8, 128), AXES, 0, 0).reshape(1024, 128)
    recv2 = lax.ppermute(recv, "c", flip)
    vm = pl.BlockSpec(memory_space=pltpu.VMEM)
    sm = pl.BlockSpec(memory_space=pltpu.SMEM)
    rows = pl.pallas_call(
        gram_kernel,
        in_specs=[sm, sm] + [vm] * 6,
        out_specs=vm,
        scratch_shapes=[
            pltpu.VMEM((1024, 128), F32),
            pltpu.VMEM((768, 128), F32),
            pltpu.VMEM((384, 128), F32),
            pltpu.VMEM((128, 128), F32),
            pltpu.VMEM((256, 3840), BF16),
            pltpu.VMEM((128, 128), F32),
        ],
        out_shape=jax.ShapeDtypeStruct((4, 32, 128), F32),
        compiler_params=pltpu.CompilerParams(vmem_limit_bytes=48 * 2**20),
        name="gram",
    )(tile_ids, table, got, keep, recv, keep2, recv2, cell_area)
    line = jnp.sum(lax.all_to_all(rows, ("xh", "xl"), 0, 0), axis=0)
    spread = jnp.broadcast_to(line[None], (16, 32, 128))
    return jnp.sum(lax.all_to_all(spread, ("y", "z"), 0, 0), axis=0) / (96 * SAMP * SAMP)


def solution(mesh):
    fine = Mesh(mesh.devices.reshape(4, 4, 2, 2, 2), AXES)
    tm = ("xl", "c")
    placed = (P(("y", "z", "xh"), tm, None), P(), P(), P())
    return jax.shard_map(body, mesh=fine, in_specs=placed, out_specs=P(tm, None), check_vma=False)
```

```python
import functools

import jax
import jax.numpy as jnp
import ml_dtypes
import numpy as np
from jax import lax
from jax.experimental import pallas as pl
from jax.experimental.pallas import tpu as pltpu
from jax.sharding import Mesh
from jax.sharding import PartitionSpec as P

STRIDE = 4
STEPS = 4
TILE = 192
CELLS = TILE * TILE
SAMP = TILE // STRIDE
AXES = ("y", "z", "xh", "xl", "c")
PAD = 640
SB = 32
PARTS = 4
PART = CELLS // PARTS
VMEM_LIMIT = 60 * 2**20
F32 = jnp.float32
BF16 = jnp.bfloat16


def stencil():
    k = np.zeros((9, 9))
    k[4, 4] = 1.0
    for step in range(STEPS):
        c = 0.12 + 0.1 * step / max(STEPS - 1, 1)
        p = np.pad(k, 1)
        lap = p[:-2, 1:-1] + p[2:, 1:-1] + p[1:-1, :-2] + p[1:-1, 2:] - 4 * k
        k = k + c * lap
    return k[4:, 4:]


K = stencil()


def coef(d, m):
    return float(K[d, m]) if d + m <= STEPS else 0.0


CORNER = coef(2, 2) / 2.0
NEAR = {1: 0, 0: 1, 2: 1, 3: 2}
FAR = {1: 4, 0: 3, 2: 3, 3: 9}


def lane_tables():
    lane = np.arange(128) % 4
    near = np.array([[coef(d, NEAR[l]) for l in lane] for d in range(5)])
    far = np.array([[coef(d, FAR[l]) for l in lane] for d in range(2)])
    return np.concatenate([near, far, np.zeros((1, 128))]).astype(np.float32)


def edge_coef(high, flip, depth, pos):
    m = NEAR[(pos % 4) if not flip else ((3 - pos) % 4)]
    return coef(depth + 2 + high, m)


def row_edge_table():
    out = np.zeros((16, 128))
    for high in range(2):
        for flip in range(2):
            for depth in range(3):
                for lane in range(128):
                    out[(2 * high + flip) * 4 + depth, lane] = edge_coef(high, flip, depth, lane)
    return out.astype(np.float32)


def col_lanes():
    where = {}
    for k in range(8):
        for par in range(2):
            for depth in range(3):
                where[((0 if par == 0 else 64) + depth + 6 * k) % 128] = (2 * k + par, 2, depth)
                where[((63 if par == 0 else 127) - depth + 6 * k) % 128] = (2 * k + par, 3, depth)
    return where


def col_edge_table():
    out = np.zeros((8, 128))
    for lane, (row, edge, depth) in col_lanes().items():
        for high in range(2):
            for flip in range(2):
                out[(edge - 2) * 4 + 2 * high + flip, lane] = edge_coef(high, flip, depth, row)
    return out.astype(np.float32)


def place(lanes, pos, j, value=1.0):
    lanes[pos, j] = value


def sum_matrix():
    s = np.zeros((384, SAMP))
    for c in range(TILE):
        for j in range(SAMP):
            d = abs(c - (4 * j + 1))
            if 3 <= d <= 4:
                s[c, j] = 1.0
            if d <= 2:
                s[192 + c, j] = 1.0
    return s


def quad_matrices():
    s = sum_matrix()
    a = np.zeros((4, 384, 256))
    b = np.zeros((4, 384, 256))
    for q in range(4):
        a[q, :, 48 * q : 48 * q + 48] = s
        a[q, :, 192 + q] = s[:, 0]
        a[q, :, 196 + q] = s[:, SAMP - 1]
        b[q, :, 64 + 48 * q : 64 + 48 * q + 48] = s
        b[q, :, q] = s[:, 0]
        b[q, :, 4 + q] = s[:, SAMP - 1]
    both = np.stack([a.reshape(1536, 256), b.reshape(1536, 256)])
    return both.astype(ml_dtypes.bfloat16)


def row_edge_matrix():
    m = np.zeros((256, 128))
    for pos in range(TILE):
        for j in range(SAMP):
            if abs(pos - (4 * j + 1)) <= 2:
                m[pos, j] = 1.0
            if abs((TILE - 1 - pos) - (4 * j + 1)) <= 2:
                m[pos, 64 + j] = 1.0
    for k in range(2):
        m[192 + k, 48 + k] = 1.0
        m[192 + k, 112 + k] = 1.0
    return m.astype(ml_dtypes.bfloat16)


def col_edge_matrix():
    m = np.zeros((12, 128, 256))
    for group in range(12):
        for lane, (row, edge, _) in col_lanes().items():
            pos = 16 * group + row
            for j in range(SAMP):
                if abs(pos - (4 * j + 1)) <= 2:
                    m[group, lane, (edge - 2) * 128 + j] = 1.0
                if abs((TILE - 1 - pos) - (4 * j + 1)) <= 2:
                    m[group, lane, (edge - 2) * 128 + 64 + j] = 1.0
    return m.reshape(1536, 256).astype(ml_dtypes.bfloat16)


def inner_mask():
    m = np.zeros((8, 384))
    for g in range(6):
        for lane in range(384):
            r, j = 8 * g + lane // 48, lane % 48
            m[g, lane] = float(0 < r < SAMP - 1 and 0 < j < SAMP - 1)
    return m.astype(np.float32)


def halves(v):
    hi = v.astype(BF16)
    return hi, (v - hi.astype(F32)).astype(BF16)


def lanes_of(shape):
    return lax.broadcasted_iota(jnp.int32, shape, len(shape) - 1)


def space_index():
    return lax.axis_index("y") * 8 + lax.axis_index("z") * 2 + lax.axis_index("xh")


def swap_ends(v, lane):
    return jnp.where(
        lane == 0,
        pltpu.roll(v, 128 - (SAMP - 1), 1),
        jnp.where(lane == SAMP - 1, pltpu.roll(v, SAMP - 1, 1), v),
    )


def filter_kernel(
    ids, table, x_hbm, area_hbm, quad_hbm, colm_hbm, rowm_ref, small_ref, mask_ref,
    keep_ref, send_ref, edge_ref, areas_ref,
    xs, area, quads, colm, wp, lhs, stage, root, packed, lrow, lcol, strip, sem_x, sem_a, sem_c,
):
    xl = lax.axis_index("xl")
    lane = lanes_of((SB, 128))
    first_slot = 3 * space_index()

    def copy_x(tile, part):
        at = pl.ds(part * PART, PART)
        return pltpu.make_async_copy(x_hbm.at[tile, :, at], xs.at[tile, :, at], sem_x.at[tile * PARTS + part])

    def copy_area(part):
        at = pl.ds(part * PART, PART)
        return pltpu.make_async_copy(area_hbm.at[:, at], area.at[:, at], sem_a.at[part])

    copy_quads = pltpu.make_async_copy(quad_hbm, quads, sem_c.at[0])
    copy_colm = pltpu.make_async_copy(colm_hbm, colm, sem_c.at[1])
    for part in range(2):
        copy_area(part).start()
        copy_x(0, part).start()
    wp[:, :PAD] = jnp.zeros((SB, PAD), F32)
    wp[:, PAD + CELLS :] = jnp.zeros((SB, 512), F32)
    strip[:, 96:, :] = jnp.zeros((8, 32, 128), F32)
    stage[...] = jnp.zeros((2, 2, 16, 1536), F32)
    wide = lambda k: jnp.concatenate([k, k], axis=1)
    near = [wide(small_ref[d : d + 1, :]) for d in range(5)]
    far = [wide(small_ref[5 + d : 6 + d, :]) for d in range(2)]
    lane2 = lanes_of((SB, 256))
    lane_one = lanes_of((1, 256))
    picked = (lane_one >= 64) & (lane_one % 4 == 1)

    def win(off):
        return wp[:, PAD + off : PAD + off + 256]

    def collect(tile):
        if tile == 0:
            copy_quads.wait()
        outs, area_outs = [], []
        for n in range(2):
            v = stage[tile % 2, n]
            hi = v.astype(BF16)
            rest = v - hi.astype(F32)
            mid = rest.astype(BF16)
            lhs[tile % 2, n, 384:400, :] = hi
            lhs[tile % 2, n, 400:416, :] = mid
            lhs[tile % 2, n, 416:432, :] = (rest - mid.astype(F32)).astype(BF16)
            o = jnp.dot(lhs[tile % 2, n], quads[n], preferred_element_type=F32)
            outs.append(o[:192] + o[192:384])
            area_outs.append(o[384:392] + o[400:408] + o[416:424])
        out_a, out_b = outs
        a, b = area_outs
        lane8 = lanes_of((8, 128))
        mean = jnp.concatenate([a[:, :128], jnp.where(lane8 < 64, a[:, 128:], b[:, :128]), b[:, 128:]], axis=1)
        inner = mask_ref[...] > 0.0
        root[...] = jnp.where(inner, lax.rsqrt(jnp.where(inner, mean, 1.0)), 0.0)

        left = jnp.zeros((SB, 128), F32)
        right = jnp.zeros((SB, 128), F32)
        for g in range(6):
            a, b = out_a[SB * g : SB * g + SB], out_b[SB * g : SB * g + SB]
            a1, b0 = a[:, 128:], b[:, :128]
            packed[g, :, 0:128] = a[:, :128] * root[g : g + 1, 0:128]
            packed[g, :, 128:256] = jnp.where(lane < 64, a1, b0) * root[g : g + 1, 128:256]
            packed[g, :, 256:384] = b[:, 128:] * root[g : g + 1, 256:384]
            at_a = (lane >= 8 * g) & (lane < 8 * g + 4)
            at_b = (lane >= 8 * g + 4) & (lane < 8 * g + 8)
            left = jnp.where(at_a, pltpu.roll(a1, (8 * g + 64) % 128, 1), left)
            left = jnp.where(at_b, pltpu.roll(b0, (8 * g + 4) % 128, 1), left)
            right = jnp.where(at_a, pltpu.roll(a1, (8 * g + 60) % 128, 1), right)
            right = jnp.where(at_b, b0 if g == 0 else pltpu.roll(b0, 8 * g, 1), right)
        keep_ref[3 * tile : 3 * tile + 3] = packed[pl.ds(3 * xl, 3)]
        send_ref[3 * tile : 3 * tile + 3] = packed[pl.ds(3 * (1 - xl), 3)]
        here = slice(32 * tile, 32 * tile + 32)
        strip[4, here, :] = out_a[:SB, :128]
        strip[5, here, :] = swap_ends(pltpu.roll(out_b[160:192, 128:], 48, 1), lane)
        strip[6, here, :] = left
        strip[7, here, :] = swap_ends(right, lane)


    for tile in range(3):
        slot = first_slot + tile
        aid = ids[slot] % 16
        area8 = pl.multiple_of((aid // 8) * 8, 8)
        turn = (8 - aid % 8) % 8
        row0 = tile * 32

        def area_row(off, size):
            return pltpu.roll(area[pl.ds(area8, 8), off : off + size], turn, 0)[0:1]

        def variant(edge):
            return (table[1, edge, slot] & 1) * 2 + table[2, edge, slot]

        k2 = small_ref[pl.ds(24 + variant(2), 1), :] + small_ref[pl.ds(28 + variant(3), 1), :]

        for q in range(PARTS):
            if tile == 0:
                copy_area(q).wait()
            copy_x(tile, q).wait()
            if tile == 0 and q + 2 < PARTS:
                copy_area(q + 2).start()
                copy_x(0, q + 2).start()
            if q == 1 and tile == 0:
                copy_quads.start()
            if q == 1 and tile < 2:
                for n in range(PARTS):
                    copy_x(tile + 1, n).start()
            if q == 1 and tile == 1:
                copy_colm.start()
            for g in range(3 * q, 3 * q + 3):
                acc = None
                for k in range(8):
                    vs = []
                    for part in range(3):
                        off = g * 3072 + (3 * k + part) * 128
                        w = xs[tile, :, off : off + 128] * area_row(off, 128)
                        wp[:, PAD + off : PAD + off + 128] = w
                        vs.append(w)
                    both = jnp.where(lane < 3, vs[0], jnp.where(lane >= 125, vs[2], vs[1]))
                    if k == 0:
                        acc = both
                    else:
                        moved = pltpu.roll(both, 6 * k, 1)
                        mine = ((lane >= 6 * k - 3) & (lane < 6 * k + 3)) | ((lane >= 61 + 6 * k) & (lane < 67 + 6 * k))
                        acc = jnp.where(mine, moved, acc)
                hi, lo = halves(acc * k2)
                lcol[row0 : row0 + SB, g * 128 : g * 128 + 128] = hi
                lcol[96 + row0 : 96 + row0 + SB, g * 128 : g * 128 + 128] = lo

            if q == 1 and tile > 0:
                collect(tile - 1)
            for r in range(max(0, 12 * q - 1), 12 * q + 11 if q < PARTS - 1 else SAMP):
                g, h = r // 8, r % 8
                base = 768 * r
                s0 = win(base + 128)
                s1 = win(base + 384) + win(base)
                s2 = win(base + 512) + win(base - 256)
                s3 = win(base + 768) + win(base - 384)
                s4 = win(base + 896) + win(base - 640)
                va = near[0] * s0 + near[2] * s2 + near[4] * s4
                vb = near[1] * s1 + near[3] * s3
                v1 = va + pltpu.roll(vb, 64, 1)
                v2 = far[1] * s1 + pltpu.roll(far[0] * s0, 192, 1)
                parts = [v2[:, :128], jnp.where(lane < 64, v2[:, 128:], v1[:, :128]), v1[:, 128:]]
                for p, v in enumerate(parts):
                    hi, lo = halves(v)
                    at = (h % 4) * 384 + p * 128
                    lhs[tile % 2, h // 4, g * SB : g * SB + SB, at : at + 128] = hi
                    lhs[tile % 2, h // 4, 192 + g * SB : 192 + g * SB + SB, at : at + 128] = lo
                at = (h % 4) * 384 + 128
                stage[tile % 2, h // 4, g : g + 1, at : at + 256] = jnp.where(picked, area_row(base + 128, 256), 0.0)

        for edge in range(2):
            if edge == 0:
                lines = [win(0), pltpu.roll(win(128), 192, 1), win(384)]
            else:
                lines = [pltpu.roll(win(36608), 192, 1), win(36480), pltpu.roll(win(36224), 192, 1)]
            v = variant(edge) * 4
            u = jnp.zeros((SB, 256), F32)
            for d in range(3):
                u = u + wide(small_ref[pl.ds(8 + v + d, 1), :]) * lines[d]
            first, second = lines[0][:, :128], lines[0][:, 128:]
            u1 = jnp.where(
                lane == 64,
                pltpu.roll(first, 64, 1) * CORNER,
                jnp.where(lane == 65, pltpu.roll(second, 2, 1) * CORNER, u[:, 128:]),
            )
            for p, v in enumerate((u[:, :128], u1)):
                hi, lo = halves(v)
                at = edge * 96 + row0
                lrow[at : at + SB, 128 * p : 128 * p + 128] = hi
                lrow[192 + at : 192 + at + SB, 128 * p : 128 * p + 128] = lo

    collect(2)
    copy_colm.wait()
    cr = jnp.dot(lrow[...], rowm_ref[...], preferred_element_type=F32)
    cc = jnp.dot(lcol[...], colm[...], preferred_element_type=F32)
    cr = cr[:192] + cr[192:]
    cc = cc[:96] + cc[96:]
    given = [cr[:96], cr[96:], cc[:, :128], cc[:, 128:]]
    for edge in range(4):
        for t in range(3):
            slot = first_slot + t
            v = given[edge][32 * t : 32 * t + 32]
            v = jnp.where(table[2, edge, slot] == 1, pltpu.roll(v, 64, 1), v)
            strip[edge, 32 * t : 32 * t + 32, :] = jnp.where(table[1, edge, slot] & 1 == 1, swap_ends(v, lane), v)
    turned = []
    for q in range(8):
        tr = jnp.transpose(strip[q])
        edge_ref[pl.ds(q, SAMP, stride=8), :] = tr[:SAMP]
        if q < 2:
            turned.append([tr[48:49], tr[49:50]])
    lane1 = lanes_of((1, 128))
    edge_ref[6:7, :] = turned[0][0]
    edge_ref[7:8, :] = turned[0][1]
    for end in range(2):
        for t in range(3):
            at = 3 * end + t
            moved = pltpu.roll(turned[1][end], 96 - 32 * t, 1)
            edge_ref[at : at + 1, :] = jnp.where(lane1 >= 96, moved, edge_ref[at : at + 1, :])

    chip = space_index() * 2 + xl
    ends = (chip == 0) | (chip == SAMP - 1)
    place = jnp.minimum(chip, SAMP - 1)
    cell = 4 * place + 1
    swap = 4 * jnp.where(ends, SAMP - 1 - place, place) + 1
    lane16 = lanes_of((16, 128))
    for e, spot in enumerate((192 + cell, 189 * 192 + swap, cell * 192 + 1, cell * 192 + 189)):
        a = area[:, pl.ds(pl.multiple_of((spot // 128) * 128, 128), 128)]
        a = jnp.sum(jnp.where(lane16 == spot % 128, a, 0.0), axis=1, keepdims=True)
        v = jnp.broadcast_to(lax.rsqrt(a), (16, 128))
        if e >= 2:
            v = jnp.where(ends, 0.0, v)
        areas_ref[16 * e : 16 * e + 16, :] = v


def inner_kernel(keep_ref, recv_ref, keep2_ref, recv2_ref, out_ref, hl):
    xl, c = lax.axis_index("xl"), lax.axis_index("c")
    for ref, row in (
        (keep_ref, 2 * xl + c),
        (recv_ref, 2 * (1 - xl) + c),
        (keep2_ref, 2 * xl + 1 - c),
        (recv2_ref, 2 * (1 - xl) + 1 - c),
    ):
        at = pl.multiple_of(row * 32, 32)
        for b in range(9):
            hi, lo = halves(ref[b])
            hl[pl.ds(at, 32), 384 * b : 384 * b + 384] = hi
            hl[pl.ds(pl.multiple_of(128 + at, 32), 32), 384 * b : 384 * b + 384] = lo
    out_ref[...] = self_product(hl[...])


def self_product(hl):
    g = lax.dot_general(hl[:128], hl, (((1,), (1,)), ((), ())), preferred_element_type=F32)
    cross = g[:, 128:]
    return g[:, :128] + cross + jnp.transpose(cross)


def edge_kernel(ids_ref, table_ref, got_ref, got2_ref, areas, inner_ref, out_ref, z, near, sel, full):
    xl, c = lax.axis_index("xl"), lax.axis_index("c")
    chip = space_index() * 2 + xl
    first, last = chip == 0, chip == SAMP - 1
    lane = lanes_of((8, 128))
    full[...] = inner_ref[...]

    @pl.when(chip < SAMP)
    def _():
        even = c == 0
        for s in range(32):
            v = []
            for x in range(2):
                at = s * 16 + 8 * x
                mine, other = got_ref[at : at + 8, :], got2_ref[at : at + 8, :]
                v += [jnp.where(even, mine, other), jnp.where(even, other, mine)]
            for i in range(4):
                acc = v[i]
                for t in range(4):
                    if t != i:
                        acc = jnp.where(lane // 32 == t, pltpu.roll(v[t], (32 * (t - i)) % 128, 1), acc)
                at = s * 24 + 8 * i if i < 3 else 768 + s * 8
                z[at : at + 8, :] = acc

        near[...] = jnp.full((16, 128), -1, jnp.int32)
        for k in range(3):
            near[4 * k : 4 * k + 4, :96] = table_ref[k]
        near[12:13, :96] = ids_ref[...] % 16
        lane1 = lanes_of((1, 128))
        used = lane1 < 96

        def line(k, e):
            return near[4 * k + e : 4 * k + e + 1, :]

        none = jnp.full((1, 128), -1, jnp.int32)
        pos = [jnp.where(used, line(0, e) * 8 + line(1, e), -1) for e in range(4)]
        own = [jnp.where(used, lane1 * 8 + 4 + e, -1) for e in range(4)]
        near[13:15, :] = jnp.full((2, 128), -1, jnp.int32)

        @pl.when(first)
        def _():
            sub = lax.broadcasted_iota(jnp.int32, (128, 128), 0)
            for n, edge in enumerate((0, 2)):
                n1, e1, f1 = line(0, edge), line(1, edge), line(2, edge)
                side = 2 * (1 - (e1 >> 1)) + f1
                found = jnp.zeros((16, 128), F32)
                for e in range(4):
                    one = jnp.where((sub == n1) & (side == e), 1.0, 0.0).astype(BF16)
                    rows = jnp.concatenate([line(0, e), line(1, e), line(2, e), jnp.zeros((13, 128), jnp.int32)], axis=0)
                    rows = jnp.where(lanes_of((16, 128)) < 96, rows, 0).astype(F32).astype(BF16)
                    found = found + jnp.dot(rows, one, preferred_element_type=F32)
                found = found.astype(jnp.int32)
                n2, e2, f2 = found[0:1], found[1:2], found[2:3]
                b2 = (e1 & 1) ^ f2
                row = jnp.where(e2 < 2, e2, b2)
                col = jnp.where(e2 < 2, b2, e2 - 2)
                s2 = (n2 * 43) >> 7
                spare = 768 + s2 * 8 + 3 * col + (n2 - 3 * s2)
                near[13 + n : 14 + n, :] = jnp.where(used, jnp.where(row == 0, n2 * 8 + 6 + col, spare), -1)

        more0 = jnp.where(first, pos[2], jnp.where(last, pos[3], none))
        more1 = jnp.where(first, pos[3], jnp.where(last, pos[2], none))
        picks = [
            [own[0], pos[0], more0, near[13:14, :], near[14:15, :]],
            [own[1], pos[1], more1],
            [own[2], pos[2]],
            [own[3], pos[3]],
        ]
        sub = lax.broadcasted_iota(jnp.int32, (128, 128), 0)
        for block in range(8):
            at = sub + 128 * block
            for e in range(4):
                total = jnp.zeros((128, 128), F32)
                for p in picks[e]:
                    total = total + jnp.where(at == p, 1.0, 0.0)
                sel[128 * block : 128 * block + 128, 128 * e : 128 * e + 128] = total.astype(BF16)
        sub16 = lax.broadcasted_iota(jnp.int32, (16, 128), 0)
        mine = sub16 == near[12:13, :]
        weight = [jnp.sum(jnp.where(mine, areas[16 * e : 16 * e + 16, :], 0.0), axis=0, keepdims=True) for e in range(4)]
        turned = jnp.concatenate([jnp.transpose(z[128 * b : 128 * b + 128, :]) for b in range(8)], axis=1)
        hi, lo = halves(turned)
        both = jnp.dot(jnp.concatenate([hi, lo], axis=0), sel[...], preferred_element_type=F32)
        hi, lo = halves((both[:128] + both[128:]) * jnp.concatenate(weight, axis=1))
        full[...] += self_product(jnp.concatenate([hi, lo], axis=0))

    for k in range(2):
        block = full[pl.ds(pl.multiple_of(64 * k + 32 * c, 32), 32), :]
        out_ref[k] = block
        out_ref[2 + k] = block


def body(pw_field, cell_area, tile_ids, edge_table):
    table = jnp.transpose(edge_table, (0, 2, 1))
    small = jnp.asarray(np.concatenate([lane_tables(), row_edge_table(), col_edge_table()]))
    vm = pl.BlockSpec(memory_space=pltpu.VMEM)
    sm = pl.BlockSpec(memory_space=pltpu.SMEM)
    hbm = pl.BlockSpec(memory_space=pl.ANY)
    keep, send, edges, areas = pl.pallas_call(
        filter_kernel,
        in_specs=[sm, sm] + [hbm] * 4 + [vm] * 3,
        out_specs=[vm] * 4,
        scratch_shapes=[
            pltpu.VMEM((3, SB, CELLS), F32),
            pltpu.VMEM((16, CELLS), F32),
            pltpu.VMEM((2, 1536, 256), BF16),
            pltpu.VMEM((1536, 256), BF16),
            pltpu.VMEM((SB, PAD + CELLS + 512), F32),
            pltpu.VMEM((2, 2, 432, 1536), BF16),
            pltpu.VMEM((2, 2, 16, 1536), F32),
            pltpu.VMEM((8, 384), F32),
            pltpu.VMEM((6, SB, 384), F32),
            pltpu.VMEM((384, 256), BF16),
            pltpu.VMEM((192, 1536), BF16),
            pltpu.VMEM((8, 128, 128), F32),
            pltpu.SemaphoreType.DMA((3 * PARTS,)),
            pltpu.SemaphoreType.DMA((PARTS,)),
            pltpu.SemaphoreType.DMA((2,)),
        ],
        out_shape=[
            jax.ShapeDtypeStruct((9, 32, 384), F32),
            jax.ShapeDtypeStruct((9, 32, 384), F32),
            jax.ShapeDtypeStruct((512, 128), F32),
            jax.ShapeDtypeStruct((64, 128), F32),
        ],
        compiler_params=pltpu.CompilerParams(vmem_limit_bytes=VMEM_LIMIT),
        name="filter",
    )(
        tile_ids, table, pw_field, cell_area, jnp.asarray(quad_matrices()), jnp.asarray(col_edge_matrix()),
        jnp.asarray(row_edge_matrix()), small, jnp.asarray(inner_mask()),
    )

    flip = [(0, 1), (1, 0)]
    recv = lax.ppermute(send, "xl", flip)
    keep2 = lax.ppermute(keep, "c", flip)
    got = lax.all_to_all(edges.reshape(64, 8, 128), AXES[:4], 0, 0).reshape(512, 128)
    got2 = lax.ppermute(got, "c", flip)
    recv2 = lax.ppermute(recv, "c", flip)
    inner = pl.pallas_call(
        inner_kernel,
        in_specs=[vm] * 4,
        out_specs=vm,
        scratch_shapes=[pltpu.VMEM((256, 3456), BF16)],
        out_shape=jax.ShapeDtypeStruct((128, 128), F32),
        compiler_params=pltpu.CompilerParams(vmem_limit_bytes=VMEM_LIMIT),
        name="inner",
    )(keep, recv, keep2, recv2)
    rows = pl.pallas_call(
        edge_kernel,
        in_specs=[vm] * 6,
        out_specs=vm,
        scratch_shapes=[
            pltpu.VMEM((1024, 128), F32),
            pltpu.VMEM((16, 128), jnp.int32),
            pltpu.VMEM((1024, 512), BF16),
            pltpu.VMEM((128, 128), F32),
        ],
        out_shape=jax.ShapeDtypeStruct((4, 32, 128), F32),
        compiler_params=pltpu.CompilerParams(vmem_limit_bytes=VMEM_LIMIT),
        name="edge",
    )(tile_ids.reshape(1, 96), table, got, got2, areas, inner)
    line = jnp.sum(lax.all_to_all(rows, ("xh", "xl"), 0, 0), axis=0)
    spread = jnp.broadcast_to(line[None], (16, 32, 128))
    return jnp.sum(lax.all_to_all(spread, ("y", "z"), 0, 0), axis=0) / (96 * SAMP * SAMP)


def solution(mesh):
    fine = Mesh(mesh.devices.reshape(4, 4, 2, 2, 2), AXES)
    tm = ("xl", "c")
    placed = (P(("y", "z", "xh"), tm, None), P(), P(), P())
    return jax.shard_map(body, mesh=fine, in_specs=placed, out_specs=P(tm, None), check_vma=False)
```

```python
import functools

import jax
import jax.numpy as jnp
import ml_dtypes
import numpy as np
from jax import lax
from jax.experimental import pallas as pl
from jax.experimental.pallas import tpu as pltpu
from jax.sharding import Mesh
from jax.sharding import PartitionSpec as P

STRIDE = 4
STEPS = 4
TILE = 192
CELLS = TILE * TILE
SAMP = TILE // STRIDE
AXES = ("y", "z", "xh", "xl", "c")
PAD = 640
SB = 32
PARTS = 4
PART = CELLS // PARTS
VMEM_LIMIT = 60 * 2**20
F32 = jnp.float32
BF16 = jnp.bfloat16


def stencil():
    k = np.zeros((9, 9))
    k[4, 4] = 1.0
    for step in range(STEPS):
        c = 0.12 + 0.1 * step / max(STEPS - 1, 1)
        p = np.pad(k, 1)
        lap = p[:-2, 1:-1] + p[2:, 1:-1] + p[1:-1, :-2] + p[1:-1, 2:] - 4 * k
        k = k + c * lap
    return k[4:, 4:]


K = stencil()


def coef(d, m):
    return float(K[d, m]) if d + m <= STEPS else 0.0


CORNER = coef(2, 2) / 2.0
NEAR = {1: 0, 0: 1, 2: 1, 3: 2}
FAR = {1: 4, 0: 3, 2: 3, 3: 9}


def lane_tables():
    lane = np.arange(128) % 4
    near = np.array([[coef(d, NEAR[l]) for l in lane] for d in range(5)])
    far = np.array([[coef(d, FAR[l]) for l in lane] for d in range(2)])
    return np.concatenate([near, far, np.zeros((1, 128))]).astype(np.float32)


def edge_coef(high, flip, depth, pos):
    m = NEAR[(pos % 4) if not flip else ((3 - pos) % 4)]
    return coef(depth + 2 + high, m)


def row_edge_table():
    out = np.zeros((16, 128))
    for high in range(2):
        for flip in range(2):
            for depth in range(3):
                for lane in range(128):
                    out[(2 * high + flip) * 4 + depth, lane] = edge_coef(high, flip, depth, lane)
    return out.astype(np.float32)


def col_lanes():
    where = {}
    for k in range(8):
        for par in range(2):
            for depth in range(3):
                where[((0 if par == 0 else 64) + depth + 6 * k) % 128] = (2 * k + par, 2, depth)
                where[((63 if par == 0 else 127) - depth + 6 * k) % 128] = (2 * k + par, 3, depth)
    return where


def col_edge_table():
    out = np.zeros((8, 128))
    for lane, (row, edge, depth) in col_lanes().items():
        for high in range(2):
            for flip in range(2):
                out[(edge - 2) * 4 + 2 * high + flip, lane] = edge_coef(high, flip, depth, row)
    return out.astype(np.float32)


def place(lanes, pos, j, value=1.0):
    lanes[pos, j] = value


def sum_matrix():
    s = np.zeros((384, SAMP))
    for c in range(TILE):
        for j in range(SAMP):
            d = abs(c - (4 * j + 1))
            if 3 <= d <= 4:
                s[c, j] = 1.0
            if d <= 2:
                s[192 + c, j] = 1.0
    return s


def quad_matrices():
    s = sum_matrix()
    a = np.zeros((4, 384, 256))
    b = np.zeros((4, 384, 256))
    for q in range(4):
        a[q, :, 48 * q : 48 * q + 48] = s
        a[q, :, 192 + q] = s[:, 0]
        a[q, :, 196 + q] = s[:, SAMP - 1]
        b[q, :, 64 + 48 * q : 64 + 48 * q + 48] = s
        b[q, :, q] = s[:, 0]
        b[q, :, 4 + q] = s[:, SAMP - 1]
    both = np.stack([a.reshape(1536, 256), b.reshape(1536, 256)])
    return both.astype(ml_dtypes.bfloat16)


def row_edge_matrix():
    m = np.zeros((256, 128))
    for pos in range(TILE):
        for j in range(SAMP):
            if abs(pos - (4 * j + 1)) <= 2:
                m[pos, j] = 1.0
            if abs((TILE - 1 - pos) - (4 * j + 1)) <= 2:
                m[pos, 64 + j] = 1.0
    for k in range(2):
        m[192 + k, 48 + k] = 1.0
        m[192 + k, 112 + k] = 1.0
    return m.astype(ml_dtypes.bfloat16)


def col_edge_matrix():
    m = np.zeros((12, 128, 256))
    for group in range(12):
        for lane, (row, edge, _) in col_lanes().items():
            pos = 16 * group + row
            for j in range(SAMP):
                if abs(pos - (4 * j + 1)) <= 2:
                    m[group, lane, (edge - 2) * 128 + j] = 1.0
                if abs((TILE - 1 - pos) - (4 * j + 1)) <= 2:
                    m[group, lane, (edge - 2) * 128 + 64 + j] = 1.0
    return m.reshape(1536, 256).astype(ml_dtypes.bfloat16)


def inner_mask():
    m = np.zeros((8, 384))
    for g in range(6):
        for lane in range(384):
            r, j = 8 * g + lane // 48, lane % 48
            m[g, lane] = float(0 < r < SAMP - 1 and 0 < j < SAMP - 1)
    return m.astype(np.float32)


def halves(v):
    hi = v.astype(BF16)
    return hi, (v - hi.astype(F32)).astype(BF16)


def lanes_of(shape):
    return lax.broadcasted_iota(jnp.int32, shape, len(shape) - 1)


def space_index():
    return lax.axis_index("y") * 8 + lax.axis_index("z") * 2 + lax.axis_index("xh")


def swap_ends(v, lane):
    return jnp.where(
        lane == 0,
        pltpu.roll(v, 128 - (SAMP - 1), 1),
        jnp.where(lane == SAMP - 1, pltpu.roll(v, SAMP - 1, 1), v),
    )


def filter_kernel(
    ids, table, x_hbm, area_hbm, quad_hbm, colm_hbm, rowm_ref, small_ref, mask_ref,
    keep_ref, send_ref, edge_ref, areas_ref,
    xs, area, quads, colm, wp, lhs, stage, root, packed, lrow, lcol, strip, sem_x, sem_a, sem_c,
):
    xl = lax.axis_index("xl")
    lane = lanes_of((SB, 128))
    first_slot = 3 * space_index()

    def copy_x(tile, part):
        at = pl.ds(part * PART, PART)
        return pltpu.make_async_copy(x_hbm.at[tile, :, at], xs.at[tile, :, at], sem_x.at[tile * PARTS + part])

    def copy_area(part):
        at = pl.ds(part * PART, PART)
        return pltpu.make_async_copy(area_hbm.at[:, at], area.at[:, at], sem_a.at[part])

    copy_quads = pltpu.make_async_copy(quad_hbm, quads, sem_c.at[0])
    copy_colm = pltpu.make_async_copy(colm_hbm, colm, sem_c.at[1])
    for part in range(2):
        copy_area(part).start()
        copy_x(0, part).start()
    wp[:, :PAD] = jnp.zeros((SB, PAD), F32)
    wp[:, PAD + CELLS :] = jnp.zeros((SB, 512), F32)
    strip[:, 96:, :] = jnp.zeros((8, 32, 128), F32)
    stage[...] = jnp.zeros((2, 2, 16, 1536), F32)
    wide = lambda k: jnp.concatenate([k, k], axis=1)
    near = [wide(small_ref[d : d + 1, :]) for d in range(5)]
    far = [wide(small_ref[5 + d : 6 + d, :]) for d in range(2)]
    lane2 = lanes_of((SB, 256))
    lane_one = lanes_of((1, 256))
    picked = (lane_one >= 64) & (lane_one % 4 == 1)

    def win(off):
        return wp[:, PAD + off : PAD + off + 256]

    def collect(tile):
        if tile == 0:
            copy_quads.wait()
        outs, area_outs = [], []
        for n in range(2):
            v = stage[tile % 2, n]
            hi = v.astype(BF16)
            rest = v - hi.astype(F32)
            mid = rest.astype(BF16)
            lhs[tile % 2, n, 384:400, :] = hi
            lhs[tile % 2, n, 400:416, :] = mid
            lhs[tile % 2, n, 416:432, :] = (rest - mid.astype(F32)).astype(BF16)
            o = jnp.dot(lhs[tile % 2, n], quads[n], preferred_element_type=F32)
            outs.append(o[:192] + o[192:384])
            area_outs.append(o[384:392] + o[400:408] + o[416:424])
        out_a, out_b = outs
        a, b = area_outs
        lane8 = lanes_of((8, 128))
        mean = jnp.concatenate([a[:, :128], jnp.where(lane8 < 64, a[:, 128:], b[:, :128]), b[:, 128:]], axis=1)
        inner = mask_ref[...] > 0.0
        root[...] = jnp.where(inner, lax.rsqrt(jnp.where(inner, mean, 1.0)), 0.0)

        left = jnp.zeros((SB, 128), F32)
        right = jnp.zeros((SB, 128), F32)
        for g in range(6):
            a, b = out_a[SB * g : SB * g + SB], out_b[SB * g : SB * g + SB]
            a1, b0 = a[:, 128:], b[:, :128]
            packed[g, :, 0:128] = a[:, :128] * root[g : g + 1, 0:128]
            packed[g, :, 128:256] = jnp.where(lane < 64, a1, b0) * root[g : g + 1, 128:256]
            packed[g, :, 256:384] = b[:, 128:] * root[g : g + 1, 256:384]
            at_a = (lane >= 8 * g) & (lane < 8 * g + 4)
            at_b = (lane >= 8 * g + 4) & (lane < 8 * g + 8)
            left = jnp.where(at_a, pltpu.roll(a1, (8 * g + 64) % 128, 1), left)
            left = jnp.where(at_b, pltpu.roll(b0, (8 * g + 4) % 128, 1), left)
            right = jnp.where(at_a, pltpu.roll(a1, (8 * g + 60) % 128, 1), right)
            right = jnp.where(at_b, b0 if g == 0 else pltpu.roll(b0, 8 * g, 1), right)
        keep_ref[3 * tile : 3 * tile + 3] = packed[pl.ds(3 * xl, 3)]
        send_ref[3 * tile : 3 * tile + 3] = packed[pl.ds(3 * (1 - xl), 3)]
        here = slice(32 * tile, 32 * tile + 32)
        strip[4, here, :] = out_a[:SB, :128]
        strip[5, here, :] = swap_ends(pltpu.roll(out_b[160:192, 128:], 48, 1), lane)
        strip[6, here, :] = left
        strip[7, here, :] = swap_ends(right, lane)


    for tile in range(3):
        slot = first_slot + tile
        aid = ids[slot] % 16
        area8 = pl.multiple_of((aid // 8) * 8, 8)
        turn = (8 - aid % 8) % 8
        row0 = tile * 32

        def area_row(off, size):
            return pltpu.roll(area[pl.ds(area8, 8), off : off + size], turn, 0)[0:1]

        def variant(edge):
            return (table[1, edge, slot] & 1) * 2 + table[2, edge, slot]

        k2 = small_ref[pl.ds(24 + variant(2), 1), :] + small_ref[pl.ds(28 + variant(3), 1), :]

        for q in range(PARTS):
            if tile == 0:
                copy_area(q).wait()
            copy_x(tile, q).wait()
            if tile == 0 and q + 2 < PARTS:
                copy_area(q + 2).start()
                copy_x(0, q + 2).start()
            if q == 1 and tile == 0:
                copy_quads.start()
            if q == 1 and tile < 2:
                for n in range(PARTS):
                    copy_x(tile + 1, n).start()
            if q == 1 and tile == 1:
                copy_colm.start()
            for g in range(3 * q, 3 * q + 3):
                acc = None
                for k in range(8):
                    vs = []
                    for part in range(3):
                        off = g * 3072 + (3 * k + part) * 128
                        w = xs[tile, :, off : off + 128] * area_row(off, 128)
                        wp[:, PAD + off : PAD + off + 128] = w
                        vs.append(w)
                    both = jnp.where(lane < 3, vs[0], jnp.where(lane >= 125, vs[2], vs[1]))
                    if k == 0:
                        acc = both
                    else:
                        moved = pltpu.roll(both, 6 * k, 1)
                        mine = ((lane >= 6 * k - 3) & (lane < 6 * k + 3)) | ((lane >= 61 + 6 * k) & (lane < 67 + 6 * k))
                        acc = jnp.where(mine, moved, acc)
                hi, lo = halves(acc * k2)
                lcol[row0 : row0 + SB, g * 128 : g * 128 + 128] = hi
                lcol[96 + row0 : 96 + row0 + SB, g * 128 : g * 128 + 128] = lo

            if q == 1 and tile > 0:
                collect(tile - 1)
            for r in range(max(0, 12 * q - 1), 12 * q + 11 if q < PARTS - 1 else SAMP):
                g, h = r // 8, r % 8
                base = 768 * r
                s0 = win(base + 128)
                s1 = win(base + 384) + win(base)
                s2 = win(base + 512) + win(base - 256)
                s3 = win(base + 768) + win(base - 384)
                s4 = win(base + 896) + win(base - 640)
                va = near[0] * s0 + near[2] * s2 + near[4] * s4
                vb = near[1] * s1 + near[3] * s3
                v1 = va + pltpu.roll(vb, 64, 1)
                v2 = far[1] * s1 + pltpu.roll(far[0] * s0, 192, 1)
                parts = [v2[:, :128], jnp.where(lane < 64, v2[:, 128:], v1[:, :128]), v1[:, 128:]]
                for p, v in enumerate(parts):
                    hi, lo = halves(v)
                    at = (h % 4) * 384 + p * 128
                    lhs[tile % 2, h // 4, g * SB : g * SB + SB, at : at + 128] = hi
                    lhs[tile % 2, h // 4, 192 + g * SB : 192 + g * SB + SB, at : at + 128] = lo
                at = (h % 4) * 384 + 128
                stage[tile % 2, h // 4, g : g + 1, at : at + 256] = jnp.where(picked, area_row(base + 128, 256), 0.0)

        for edge in range(2):
            if edge == 0:
                lines = [win(0), pltpu.roll(win(128), 192, 1), win(384)]
            else:
                lines = [pltpu.roll(win(36608), 192, 1), win(36480), pltpu.roll(win(36224), 192, 1)]
            v = variant(edge) * 4
            u = jnp.zeros((SB, 256), F32)
            for d in range(3):
                u = u + wide(small_ref[pl.ds(8 + v + d, 1), :]) * lines[d]
            first, second = lines[0][:, :128], lines[0][:, 128:]
            u1 = jnp.where(
                lane == 64,
                pltpu.roll(first, 64, 1) * CORNER,
                jnp.where(lane == 65, pltpu.roll(second, 2, 1) * CORNER, u[:, 128:]),
            )
            for p, v in enumerate((u[:, :128], u1)):
                hi, lo = halves(v)
                at = edge * 96 + row0
                lrow[at : at + SB, 128 * p : 128 * p + 128] = hi
                lrow[192 + at : 192 + at + SB, 128 * p : 128 * p + 128] = lo

    collect(2)
    copy_colm.wait()
    cr = jnp.dot(lrow[...], rowm_ref[...], preferred_element_type=F32)
    cc = jnp.dot(lcol[...], colm[...], preferred_element_type=F32)
    cr = cr[:192] + cr[192:]
    cc = cc[:96] + cc[96:]
    given = [cr[:96], cr[96:], cc[:, :128], cc[:, 128:]]
    for edge in range(4):
        for t in range(3):
            slot = first_slot + t
            v = given[edge][32 * t : 32 * t + 32]
            v = jnp.where(table[2, edge, slot] == 1, pltpu.roll(v, 64, 1), v)
            strip[edge, 32 * t : 32 * t + 32, :] = jnp.where(table[1, edge, slot] & 1 == 1, swap_ends(v, lane), v)
    turned = []
    for q in range(8):
        tr = jnp.transpose(strip[q])
        edge_ref[pl.ds(q, SAMP, stride=8), :] = tr[:SAMP]
        if q < 2:
            turned.append([tr[48:49], tr[49:50]])
    lane1 = lanes_of((1, 128))
    edge_ref[6:7, :] = turned[0][0]
    edge_ref[7:8, :] = turned[0][1]
    for end in range(2):
        for t in range(3):
            at = 3 * end + t
            moved = pltpu.roll(turned[1][end], 96 - 32 * t, 1)
            edge_ref[at : at + 1, :] = jnp.where(lane1 >= 96, moved, edge_ref[at : at + 1, :])

    chip = space_index() * 2 + xl
    ends = (chip == 0) | (chip == SAMP - 1)
    place = jnp.minimum(chip, SAMP - 1)
    cell = 4 * place + 1
    swap = 4 * jnp.where(ends, SAMP - 1 - place, place) + 1
    lane16 = lanes_of((16, 128))
    for e, spot in enumerate((192 + cell, 189 * 192 + swap, cell * 192 + 1, cell * 192 + 189)):
        a = area[:, pl.ds(pl.multiple_of((spot // 128) * 128, 128), 128)]
        a = jnp.sum(jnp.where(lane16 == spot % 128, a, 0.0), axis=1, keepdims=True)
        v = jnp.broadcast_to(lax.rsqrt(a), (16, 128))
        if e >= 2:
            v = jnp.where(ends, 0.0, v)
        areas_ref[16 * e : 16 * e + 16, :] = v


def inner_kernel(keep_ref, recv_ref, keep2_ref, recv2_ref, out_ref, buf, hl, sem):
    xl, c = lax.axis_index("xl"), lax.axis_index("c")
    copies = [
        pltpu.make_async_copy(ref, buf.at[n], sem.at[n])
        for n, ref in enumerate((keep_ref, recv_ref, keep2_ref, recv2_ref))
    ]
    for copy in copies:
        copy.start()
    for n, row in enumerate((2 * xl + c, 2 * (1 - xl) + c, 2 * xl + 1 - c, 2 * (1 - xl) + 1 - c)):
        copies[n].wait()
        at = pl.multiple_of(row * 32, 32)
        for b in range(9):
            hi, lo = halves(buf[n, b])
            hl[pl.ds(at, 32), 384 * b : 384 * b + 384] = hi
            hl[pl.ds(pl.multiple_of(128 + at, 32), 32), 384 * b : 384 * b + 384] = lo
    out_ref[...] = self_product(hl[...])


def self_product(hl):
    g = lax.dot_general(hl[:128], hl, (((1,), (1,)), ((), ())), preferred_element_type=F32)
    cross = g[:, 128:]
    return g[:, :128] + cross + jnp.transpose(cross)


def edge_kernel(
    ids_ref, table_ref, got_hbm, got2_hbm, areas_hbm, inner_hbm, mine_ref, other_ref,
    z, near, sel, full, got_ref, got2_ref, areas, sem,
):
    copies = [
        pltpu.make_async_copy(src, dst, sem.at[n])
        for n, (src, dst) in enumerate(((got_hbm, got_ref), (got2_hbm, got2_ref), (areas_hbm, areas), (inner_hbm, full)))
    ]
    for copy in copies:
        copy.start()
    xl, c = lax.axis_index("xl"), lax.axis_index("c")
    chip = space_index() * 2 + xl
    first, last = chip == 0, chip == SAMP - 1
    lane = lanes_of((8, 128))
    for copy in copies:
        copy.wait()

    @pl.when(chip < SAMP)
    def _():
        even = c == 0
        for s in range(32):
            v = []
            for x in range(2):
                at = s * 16 + 8 * x
                mine, other = got_ref[at : at + 8, :], got2_ref[at : at + 8, :]
                v += [jnp.where(even, mine, other), jnp.where(even, other, mine)]
            for i in range(4):
                acc = v[i]
                for t in range(4):
                    if t != i:
                        acc = jnp.where(lane // 32 == t, pltpu.roll(v[t], (32 * (t - i)) % 128, 1), acc)
                at = s * 24 + 8 * i if i < 3 else 768 + s * 8
                z[at : at + 8, :] = acc

        near[...] = jnp.full((16, 128), -1, jnp.int32)
        for k in range(3):
            near[4 * k : 4 * k + 4, :96] = table_ref[k]
        near[12:13, :96] = ids_ref[...] % 16
        lane1 = lanes_of((1, 128))
        used = lane1 < 96

        def line(k, e):
            return near[4 * k + e : 4 * k + e + 1, :]

        none = jnp.full((1, 128), -1, jnp.int32)
        pos = [jnp.where(used, line(0, e) * 8 + line(1, e), -1) for e in range(4)]
        own = [jnp.where(used, lane1 * 8 + 4 + e, -1) for e in range(4)]
        near[13:15, :] = jnp.full((2, 128), -1, jnp.int32)

        @pl.when(first)
        def _():
            sub = lax.broadcasted_iota(jnp.int32, (128, 128), 0)
            for n, edge in enumerate((0, 2)):
                n1, e1, f1 = line(0, edge), line(1, edge), line(2, edge)
                side = 2 * (1 - (e1 >> 1)) + f1
                found = jnp.zeros((16, 128), F32)
                for e in range(4):
                    one = jnp.where((sub == n1) & (side == e), 1.0, 0.0).astype(BF16)
                    rows = jnp.concatenate([line(0, e), line(1, e), line(2, e), jnp.zeros((13, 128), jnp.int32)], axis=0)
                    rows = jnp.where(lanes_of((16, 128)) < 96, rows, 0).astype(F32).astype(BF16)
                    found = found + jnp.dot(rows, one, preferred_element_type=F32)
                found = found.astype(jnp.int32)
                n2, e2, f2 = found[0:1], found[1:2], found[2:3]
                b2 = (e1 & 1) ^ f2
                row = jnp.where(e2 < 2, e2, b2)
                col = jnp.where(e2 < 2, b2, e2 - 2)
                s2 = (n2 * 43) >> 7
                spare = 768 + s2 * 8 + 3 * col + (n2 - 3 * s2)
                near[13 + n : 14 + n, :] = jnp.where(used, jnp.where(row == 0, n2 * 8 + 6 + col, spare), -1)

        more0 = jnp.where(first, pos[2], jnp.where(last, pos[3], none))
        more1 = jnp.where(first, pos[3], jnp.where(last, pos[2], none))
        picks = [
            [own[0], pos[0], more0, near[13:14, :], near[14:15, :]],
            [own[1], pos[1], more1],
            [own[2], pos[2]],
            [own[3], pos[3]],
        ]
        sub = lax.broadcasted_iota(jnp.int32, (128, 128), 0)
        for block in range(8):
            at = sub + 128 * block
            for e in range(4):
                total = jnp.zeros((128, 128), F32)
                for p in picks[e]:
                    total = total + jnp.where(at == p, 1.0, 0.0)
                sel[128 * block : 128 * block + 128, 128 * e : 128 * e + 128] = total.astype(BF16)
        sub16 = lax.broadcasted_iota(jnp.int32, (16, 128), 0)
        mine = sub16 == near[12:13, :]
        weight = [jnp.sum(jnp.where(mine, areas[16 * e : 16 * e + 16, :], 0.0), axis=0, keepdims=True) for e in range(4)]
        turned = jnp.concatenate([jnp.transpose(z[128 * b : 128 * b + 128, :]) for b in range(8)], axis=1)
        hi, lo = halves(turned)
        both = jnp.dot(jnp.concatenate([hi, lo], axis=0), sel[...], preferred_element_type=F32)
        hi, lo = halves((both[:128] + both[128:]) * jnp.concatenate(weight, axis=1))
        full[...] += self_product(jnp.concatenate([hi, lo], axis=0))

    mine_ref[...] = full[pl.ds(pl.multiple_of(64 * xl + 32 * c, 32), 32), :]
    other_ref[...] = full[pl.ds(pl.multiple_of(64 * (1 - xl) + 32 * c, 32), 32), :]


def body(pw_field, cell_area, tile_ids, edge_table):
    table = jnp.transpose(edge_table, (0, 2, 1))
    small = jnp.asarray(np.concatenate([lane_tables(), row_edge_table(), col_edge_table()]))
    vm = pl.BlockSpec(memory_space=pltpu.VMEM)
    sm = pl.BlockSpec(memory_space=pltpu.SMEM)
    hbm = pl.BlockSpec(memory_space=pl.ANY)
    keep, send, edges, areas = pl.pallas_call(
        filter_kernel,
        in_specs=[sm, sm] + [hbm] * 4 + [vm] * 3,
        out_specs=[vm] * 4,
        scratch_shapes=[
            pltpu.VMEM((3, SB, CELLS), F32),
            pltpu.VMEM((16, CELLS), F32),
            pltpu.VMEM((2, 1536, 256), BF16),
            pltpu.VMEM((1536, 256), BF16),
            pltpu.VMEM((SB, PAD + CELLS + 512), F32),
            pltpu.VMEM((2, 2, 432, 1536), BF16),
            pltpu.VMEM((2, 2, 16, 1536), F32),
            pltpu.VMEM((8, 384), F32),
            pltpu.VMEM((6, SB, 384), F32),
            pltpu.VMEM((384, 256), BF16),
            pltpu.VMEM((192, 1536), BF16),
            pltpu.VMEM((8, 128, 128), F32),
            pltpu.SemaphoreType.DMA((3 * PARTS,)),
            pltpu.SemaphoreType.DMA((PARTS,)),
            pltpu.SemaphoreType.DMA((2,)),
        ],
        out_shape=[
            jax.ShapeDtypeStruct((9, 32, 384), F32),
            jax.ShapeDtypeStruct((9, 32, 384), F32),
            jax.ShapeDtypeStruct((512, 128), F32),
            jax.ShapeDtypeStruct((64, 128), F32),
        ],
        compiler_params=pltpu.CompilerParams(vmem_limit_bytes=VMEM_LIMIT),
        name="filter",
    )(
        tile_ids, table, pw_field, cell_area, jnp.asarray(quad_matrices()), jnp.asarray(col_edge_matrix()),
        jnp.asarray(row_edge_matrix()), small, jnp.asarray(inner_mask()),
    )

    flip = [(0, 1), (1, 0)]
    recv = lax.ppermute(send, "xl", flip)
    keep2 = lax.ppermute(keep, "c", flip)
    got = lax.all_to_all(edges.reshape(64, 8, 128), AXES[:4], 0, 0).reshape(512, 128)
    got2 = lax.ppermute(got, "c", flip)
    recv2 = lax.ppermute(recv, "c", flip)
    inner = pl.pallas_call(
        inner_kernel,
        in_specs=[vm] * 4,
        out_specs=vm,
        scratch_shapes=[
            pltpu.VMEM((4, 9, 32, 384), F32),
            pltpu.VMEM((256, 3456), BF16),
            pltpu.SemaphoreType.DMA((4,)),
        ],
        out_shape=jax.ShapeDtypeStruct((128, 128), F32),
        compiler_params=pltpu.CompilerParams(vmem_limit_bytes=12 * 2**20),
        name="inner",
    )(keep, recv, keep2, recv2)
    mine, other = pl.pallas_call(
        edge_kernel,
        in_specs=[vm] * 6,
        out_specs=[vm] * 2,
        scratch_shapes=[
            pltpu.VMEM((1024, 128), F32),
            pltpu.VMEM((16, 128), jnp.int32),
            pltpu.VMEM((1024, 512), BF16),
            pltpu.VMEM((128, 128), F32),
            pltpu.VMEM((512, 128), F32),
            pltpu.VMEM((512, 128), F32),
            pltpu.VMEM((64, 128), F32),
            pltpu.SemaphoreType.DMA((4,)),
        ],
        out_shape=[jax.ShapeDtypeStruct((32, 128), F32)] * 2,
        compiler_params=pltpu.CompilerParams(vmem_limit_bytes=12 * 2**20),
        name="edge",
    )(tile_ids.reshape(1, 96), table, got, got2, areas, inner)
    across = lax.ppermute(other, ("xh", "xl"), [(0, 3), (1, 2), (2, 1), (3, 0)])
    line = mine + lax.ppermute(mine, "xh", flip) + lax.ppermute(other, "xl", flip) + across
    spread = jnp.broadcast_to(line[None], (16, 32, 128))
    return jnp.sum(lax.all_to_all(spread, ("y", "z"), 0, 0), axis=0) / (96 * SAMP * SAMP)


def solution(mesh):
    fine = Mesh(mesh.devices.reshape(4, 4, 2, 2, 2), AXES)
    tm = ("xl", "c")
    placed = (P(("y", "z", "xh"), tm, None), P(), P(), P())
    return jax.shard_map(body, mesh=fine, in_specs=placed, out_specs=P(tm, None), check_vma=False)
```

```python
import functools

import jax
import jax.numpy as jnp
import ml_dtypes
import numpy as np
from jax import lax
from jax.experimental import pallas as pl
from jax.experimental.pallas import tpu as pltpu
from jax.sharding import Mesh
from jax.sharding import PartitionSpec as P

STRIDE = 4
STEPS = 4
TILE = 192
CELLS = TILE * TILE
SAMP = TILE // STRIDE
AXES = ("y", "z", "xh", "xl", "c")
PAD = 640
SB = 32
PARTS = 4
PART = CELLS // PARTS
VMEM_LIMIT = 60 * 2**20
F32 = jnp.float32
BF16 = jnp.bfloat16


def stencil():
    k = np.zeros((9, 9))
    k[4, 4] = 1.0
    for step in range(STEPS):
        c = 0.12 + 0.1 * step / max(STEPS - 1, 1)
        p = np.pad(k, 1)
        lap = p[:-2, 1:-1] + p[2:, 1:-1] + p[1:-1, :-2] + p[1:-1, 2:] - 4 * k
        k = k + c * lap
    return k[4:, 4:]


K = stencil()


def coef(d, m):
    return float(K[d, m]) if d + m <= STEPS else 0.0


CORNER = coef(2, 2) / 2.0
NEAR = {1: 0, 0: 1, 2: 1, 3: 2}
FAR = {1: 4, 0: 3, 2: 3, 3: 9}


def lane_tables():
    lane = np.arange(128) % 4
    near = np.array([[coef(d, NEAR[l]) for l in lane] for d in range(5)])
    far = np.array([[coef(d, FAR[l]) for l in lane] for d in range(2)])
    return np.concatenate([near, far, np.zeros((1, 128))]).astype(np.float32)


def edge_coef(high, flip, depth, pos):
    m = NEAR[(pos % 4) if not flip else ((3 - pos) % 4)]
    return coef(depth + 2 + high, m)


def row_edge_table():
    out = np.zeros((16, 128))
    for high in range(2):
        for flip in range(2):
            for depth in range(3):
                for lane in range(128):
                    out[(2 * high + flip) * 4 + depth, lane] = edge_coef(high, flip, depth, lane)
    return out.astype(np.float32)


def col_lanes():
    where = {}
    for k in range(8):
        for par in range(2):
            for depth in range(3):
                where[((0 if par == 0 else 64) + depth + 6 * k) % 128] = (2 * k + par, 2, depth)
                where[((63 if par == 0 else 127) - depth + 6 * k) % 128] = (2 * k + par, 3, depth)
    return where


def col_edge_table():
    out = np.zeros((8, 128))
    for lane, (row, edge, depth) in col_lanes().items():
        for high in range(2):
            for flip in range(2):
                out[(edge - 2) * 4 + 2 * high + flip, lane] = edge_coef(high, flip, depth, row)
    return out.astype(np.float32)


def place(lanes, pos, j, value=1.0):
    lanes[pos, j] = value


def sum_matrix():
    s = np.zeros((384, SAMP))
    for c in range(TILE):
        for j in range(SAMP):
            d = abs(c - (4 * j + 1))
            if 3 <= d <= 4:
                s[c, j] = 1.0
            if d <= 2:
                s[192 + c, j] = 1.0
    return s


def quad_matrices():
    s = sum_matrix()
    a = np.zeros((4, 384, 256))
    b = np.zeros((4, 384, 256))
    for q in range(4):
        a[q, :, 48 * q : 48 * q + 48] = s
        a[q, :, 192 + q] = s[:, 0]
        a[q, :, 196 + q] = s[:, SAMP - 1]
        b[q, :, 64 + 48 * q : 64 + 48 * q + 48] = s
        b[q, :, q] = s[:, 0]
        b[q, :, 4 + q] = s[:, SAMP - 1]
    both = np.stack([a.reshape(1536, 256), b.reshape(1536, 256)])
    return both.astype(ml_dtypes.bfloat16)


def row_edge_matrix():
    m = np.zeros((256, 128))
    for pos in range(TILE):
        for j in range(SAMP):
            if abs(pos - (4 * j + 1)) <= 2:
                m[pos, j] = 1.0
            if abs((TILE - 1 - pos) - (4 * j + 1)) <= 2:
                m[pos, 64 + j] = 1.0
    for k in range(2):
        m[192 + k, 48 + k] = 1.0
        m[192 + k, 112 + k] = 1.0
    return m.astype(ml_dtypes.bfloat16)


def col_edge_matrix():
    m = np.zeros((12, 128, 256))
    for group in range(12):
        for lane, (row, edge, _) in col_lanes().items():
            pos = 16 * group + row
            for j in range(SAMP):
                if abs(pos - (4 * j + 1)) <= 2:
                    m[group, lane, (edge - 2) * 128 + j] = 1.0
                if abs((TILE - 1 - pos) - (4 * j + 1)) <= 2:
                    m[group, lane, (edge - 2) * 128 + 64 + j] = 1.0
    return m.reshape(1536, 256).astype(ml_dtypes.bfloat16)


def inner_mask():
    m = np.zeros((8, 384))
    for g in range(6):
        for lane in range(384):
            r, j = 8 * g + lane // 48, lane % 48
            m[g, lane] = float(0 < r < SAMP - 1 and 0 < j < SAMP - 1)
    return m.astype(np.float32)


def halves(v):
    hi = v.astype(BF16)
    return hi, (v - hi.astype(F32)).astype(BF16)


def lanes_of(shape):
    return lax.broadcasted_iota(jnp.int32, shape, len(shape) - 1)


def space_index():
    return lax.axis_index("y") * 8 + lax.axis_index("z") * 2 + lax.axis_index("xh")


def swap_ends(v, lane):
    return jnp.where(
        lane == 0,
        pltpu.roll(v, 128 - (SAMP - 1), 1),
        jnp.where(lane == SAMP - 1, pltpu.roll(v, SAMP - 1, 1), v),
    )


def filter_kernel(
    ids_hbm, table_hbm, x_hbm, area_hbm, quad_hbm, colm_hbm, rowm_hbm, small_hbm, mask_hbm,
    keep_ref, send_ref, edge_ref, areas_ref,
    xs, area, quads, colm, wp, lhs, stage, root, packed, lrow, lcol, strip, ids, table, rowm_ref, small_ref, mask_ref,
    sem_x, sem_a, sem_c,
):
    xl = lax.axis_index("xl")
    lane = lanes_of((SB, 128))
    first_slot = 3 * space_index()

    def copy_x(tile, part):
        at = pl.ds(part * PART, PART)
        return pltpu.make_async_copy(x_hbm.at[tile, :, at], xs.at[tile, :, at], sem_x.at[tile * PARTS + part])

    def copy_area(part):
        at = pl.ds(part * PART, PART)
        return pltpu.make_async_copy(area_hbm.at[:, at], area.at[:, at], sem_a.at[part])

    copy_quads = pltpu.make_async_copy(quad_hbm, quads, sem_c.at[0])
    copy_colm = pltpu.make_async_copy(colm_hbm, colm, sem_c.at[1])
    early = [
        pltpu.make_async_copy(src, dst, sem_c.at[2 + n])
        for n, (src, dst) in enumerate(((ids_hbm, ids), (table_hbm, table), (small_hbm, small_ref)))
    ]
    late = [
        pltpu.make_async_copy(src, dst, sem_c.at[5 + n])
        for n, (src, dst) in enumerate(((rowm_hbm, rowm_ref), (mask_hbm, mask_ref)))
    ]
    for copy in early:
        copy.start()
    for part in range(2):
        copy_area(part).start()
        copy_x(0, part).start()
    for copy in late:
        copy.start()
    wp[:, :PAD] = jnp.zeros((SB, PAD), F32)
    wp[:, PAD + CELLS :] = jnp.zeros((SB, 512), F32)
    strip[:, 96:, :] = jnp.zeros((8, 32, 128), F32)
    stage[...] = jnp.zeros((2, 2, 16, 1536), F32)
    wide = lambda k: jnp.concatenate([k, k], axis=1)
    for copy in early + late:
        copy.wait()
    near = [wide(small_ref[d : d + 1, :]) for d in range(5)]
    far = [wide(small_ref[5 + d : 6 + d, :]) for d in range(2)]
    lane2 = lanes_of((SB, 256))
    lane_one = lanes_of((1, 256))
    picked = (lane_one >= 64) & (lane_one % 4 == 1)

    def win(off):
        return wp[:, PAD + off : PAD + off + 256]

    def collect(tile):
        if tile == 0:
            copy_quads.wait()
        outs, area_outs = [], []
        for n in range(2):
            v = stage[tile % 2, n]
            hi = v.astype(BF16)
            rest = v - hi.astype(F32)
            mid = rest.astype(BF16)
            lhs[tile % 2, n, 384:400, :] = hi
            lhs[tile % 2, n, 400:416, :] = mid
            lhs[tile % 2, n, 416:432, :] = (rest - mid.astype(F32)).astype(BF16)
            o = jnp.dot(lhs[tile % 2, n], quads[n], preferred_element_type=F32)
            outs.append(o[:192] + o[192:384])
            area_outs.append(o[384:392] + o[400:408] + o[416:424])
        out_a, out_b = outs
        a, b = area_outs
        lane8 = lanes_of((8, 128))
        mean = jnp.concatenate([a[:, :128], jnp.where(lane8 < 64, a[:, 128:], b[:, :128]), b[:, 128:]], axis=1)
        inner = mask_ref[...] > 0.0
        root[...] = jnp.where(inner, lax.rsqrt(jnp.where(inner, mean, 1.0)), 0.0)

        left = jnp.zeros((SB, 128), F32)
        right = jnp.zeros((SB, 128), F32)
        for g in range(6):
            a, b = out_a[SB * g : SB * g + SB], out_b[SB * g : SB * g + SB]
            a1, b0 = a[:, 128:], b[:, :128]
            packed[g, :, 0:128] = a[:, :128] * root[g : g + 1, 0:128]
            packed[g, :, 128:256] = jnp.where(lane < 64, a1, b0) * root[g : g + 1, 128:256]
            packed[g, :, 256:384] = b[:, 128:] * root[g : g + 1, 256:384]
            at_a = (lane >= 8 * g) & (lane < 8 * g + 4)
            at_b = (lane >= 8 * g + 4) & (lane < 8 * g + 8)
            left = jnp.where(at_a, pltpu.roll(a1, (8 * g + 64) % 128, 1), left)
            left = jnp.where(at_b, pltpu.roll(b0, (8 * g + 4) % 128, 1), left)
            right = jnp.where(at_a, pltpu.roll(a1, (8 * g + 60) % 128, 1), right)
            right = jnp.where(at_b, b0 if g == 0 else pltpu.roll(b0, 8 * g, 1), right)
        keep_ref[3 * tile : 3 * tile + 3] = packed[pl.ds(3 * xl, 3)]
        send_ref[3 * tile : 3 * tile + 3] = packed[pl.ds(3 * (1 - xl), 3)]
        here = slice(32 * tile, 32 * tile + 32)
        strip[4, here, :] = out_a[:SB, :128]
        strip[5, here, :] = swap_ends(pltpu.roll(out_b[160:192, 128:], 48, 1), lane)
        strip[6, here, :] = left
        strip[7, here, :] = swap_ends(right, lane)


    for tile in range(3):
        slot = first_slot + tile
        aid = ids[slot] % 16
        area8 = pl.multiple_of((aid // 8) * 8, 8)
        turn = (8 - aid % 8) % 8
        row0 = tile * 32

        def area_row(off, size):
            return pltpu.roll(area[pl.ds(area8, 8), off : off + size], turn, 0)[0:1]

        def variant(edge):
            return (table[1, edge, slot] & 1) * 2 + table[2, edge, slot]

        k2 = small_ref[pl.ds(24 + variant(2), 1), :] + small_ref[pl.ds(28 + variant(3), 1), :]

        for q in range(PARTS):
            if tile == 0:
                copy_area(q).wait()
            copy_x(tile, q).wait()
            if tile == 0 and q + 2 < PARTS:
                copy_area(q + 2).start()
                copy_x(0, q + 2).start()
            if q == 1 and tile == 0:
                copy_quads.start()
            if q == 1 and tile < 2:
                for n in range(PARTS):
                    copy_x(tile + 1, n).start()
            if q == 1 and tile == 1:
                copy_colm.start()
            for g in range(3 * q, 3 * q + 3):
                acc = None
                for k in range(8):
                    vs = []
                    for part in range(3):
                        off = g * 3072 + (3 * k + part) * 128
                        w = xs[tile, :, off : off + 128] * area_row(off, 128)
                        wp[:, PAD + off : PAD + off + 128] = w
                        vs.append(w)
                    both = jnp.where(lane < 3, vs[0], jnp.where(lane >= 125, vs[2], vs[1]))
                    if k == 0:
                        acc = both
                    else:
                        moved = pltpu.roll(both, 6 * k, 1)
                        mine = ((lane >= 6 * k - 3) & (lane < 6 * k + 3)) | ((lane >= 61 + 6 * k) & (lane < 67 + 6 * k))
                        acc = jnp.where(mine, moved, acc)
                hi, lo = halves(acc * k2)
                lcol[row0 : row0 + SB, g * 128 : g * 128 + 128] = hi
                lcol[96 + row0 : 96 + row0 + SB, g * 128 : g * 128 + 128] = lo

            if q == 1 and tile > 0:
                collect(tile - 1)
            for r in range(max(0, 12 * q - 1), 12 * q + 11 if q < PARTS - 1 else SAMP):
                g, h = r // 8, r % 8
                base = 768 * r
                s0 = win(base + 128)
                s1 = win(base + 384) + win(base)
                s2 = win(base + 512) + win(base - 256)
                s3 = win(base + 768) + win(base - 384)
                s4 = win(base + 896) + win(base - 640)
                va = near[0] * s0 + near[2] * s2 + near[4] * s4
                vb = near[1] * s1 + near[3] * s3
                v1 = va + pltpu.roll(vb, 64, 1)
                v2 = far[1] * s1 + pltpu.roll(far[0] * s0, 192, 1)
                parts = [v2[:, :128], jnp.where(lane < 64, v2[:, 128:], v1[:, :128]), v1[:, 128:]]
                for p, v in enumerate(parts):
                    hi, lo = halves(v)
                    at = (h % 4) * 384 + p * 128
                    lhs[tile % 2, h // 4, g * SB : g * SB + SB, at : at + 128] = hi
                    lhs[tile % 2, h // 4, 192 + g * SB : 192 + g * SB + SB, at : at + 128] = lo
                at = (h % 4) * 384 + 128
                stage[tile % 2, h // 4, g : g + 1, at : at + 256] = jnp.where(picked, area_row(base + 128, 256), 0.0)

        for edge in range(2):
            if edge == 0:
                lines = [win(0), pltpu.roll(win(128), 192, 1), win(384)]
            else:
                lines = [pltpu.roll(win(36608), 192, 1), win(36480), pltpu.roll(win(36224), 192, 1)]
            v = variant(edge) * 4
            u = jnp.zeros((SB, 256), F32)
            for d in range(3):
                u = u + wide(small_ref[pl.ds(8 + v + d, 1), :]) * lines[d]
            first, second = lines[0][:, :128], lines[0][:, 128:]
            u1 = jnp.where(
                lane == 64,
                pltpu.roll(first, 64, 1) * CORNER,
                jnp.where(lane == 65, pltpu.roll(second, 2, 1) * CORNER, u[:, 128:]),
            )
            for p, v in enumerate((u[:, :128], u1)):
                hi, lo = halves(v)
                at = edge * 96 + row0
                lrow[at : at + SB, 128 * p : 128 * p + 128] = hi
                lrow[192 + at : 192 + at + SB, 128 * p : 128 * p + 128] = lo

    collect(2)
    copy_colm.wait()
    cr = jnp.dot(lrow[...], rowm_ref[...], preferred_element_type=F32)
    cc = jnp.dot(lcol[...], colm[...], preferred_element_type=F32)
    cr = cr[:192] + cr[192:]
    cc = cc[:96] + cc[96:]
    given = [cr[:96], cr[96:], cc[:, :128], cc[:, 128:]]
    for edge in range(4):
        for t in range(3):
            slot = first_slot + t
            v = given[edge][32 * t : 32 * t + 32]
            v = jnp.where(table[2, edge, slot] == 1, pltpu.roll(v, 64, 1), v)
            strip[edge, 32 * t : 32 * t + 32, :] = jnp.where(table[1, edge, slot] & 1 == 1, swap_ends(v, lane), v)
    turned = []
    for q in range(8):
        tr = jnp.transpose(strip[q])
        edge_ref[pl.ds(q, SAMP, stride=8), :] = tr[:SAMP]
        if q < 2:
            turned.append([tr[48:49], tr[49:50]])
    lane1 = lanes_of((1, 128))
    edge_ref[6:7, :] = turned[0][0]
    edge_ref[7:8, :] = turned[0][1]
    for end in range(2):
        for t in range(3):
            at = 3 * end + t
            moved = pltpu.roll(turned[1][end], 96 - 32 * t, 1)
            edge_ref[at : at + 1, :] = jnp.where(lane1 >= 96, moved, edge_ref[at : at + 1, :])

    chip = space_index() * 2 + xl
    ends = (chip == 0) | (chip == SAMP - 1)
    place = jnp.minimum(chip, SAMP - 1)
    cell = 4 * place + 1
    swap = 4 * jnp.where(ends, SAMP - 1 - place, place) + 1
    lane16 = lanes_of((16, 128))
    for e, spot in enumerate((192 + cell, 189 * 192 + swap, cell * 192 + 1, cell * 192 + 189)):
        a = area[:, pl.ds(pl.multiple_of((spot // 128) * 128, 128), 128)]
        a = jnp.sum(jnp.where(lane16 == spot % 128, a, 0.0), axis=1, keepdims=True)
        v = jnp.broadcast_to(lax.rsqrt(a), (16, 128))
        if e >= 2:
            v = jnp.where(ends, 0.0, v)
        areas_ref[16 * e : 16 * e + 16, :] = v


def inner_kernel(keep_ref, recv_ref, keep2_ref, recv2_ref, out_ref, buf, hl, sem):
    xl, c = lax.axis_index("xl"), lax.axis_index("c")
    copies = [
        pltpu.make_async_copy(ref, buf.at[n], sem.at[n])
        for n, ref in enumerate((keep_ref, recv_ref, keep2_ref, recv2_ref))
    ]
    for copy in copies:
        copy.start()
    for n, row in enumerate((2 * xl + c, 2 * (1 - xl) + c, 2 * xl + 1 - c, 2 * (1 - xl) + 1 - c)):
        copies[n].wait()
        at = pl.multiple_of(row * 32, 32)
        for b in range(9):
            hi, lo = halves(buf[n, b])
            hl[pl.ds(at, 32), 384 * b : 384 * b + 384] = hi
            hl[pl.ds(pl.multiple_of(128 + at, 32), 32), 384 * b : 384 * b + 384] = lo
    out_ref[...] = self_product(hl[...])


def self_product(hl):
    g = lax.dot_general(hl[:128], hl, (((1,), (1,)), ((), ())), preferred_element_type=F32)
    cross = g[:, 128:]
    return g[:, :128] + cross + jnp.transpose(cross)


def edge_kernel(
    ids_ref, table_ref, got_hbm, got2_hbm, areas_hbm, inner_hbm, mine_ref, other_ref,
    z, near, sel, full, got_ref, got2_ref, areas, sem,
):
    copies = [
        pltpu.make_async_copy(src, dst, sem.at[n])
        for n, (src, dst) in enumerate(((got_hbm, got_ref), (got2_hbm, got2_ref), (areas_hbm, areas), (inner_hbm, full)))
    ]
    for copy in copies:
        copy.start()
    xl, c = lax.axis_index("xl"), lax.axis_index("c")
    chip = space_index() * 2 + xl
    first, last = chip == 0, chip == SAMP - 1
    lane = lanes_of((8, 128))
    for copy in copies:
        copy.wait()

    @pl.when(chip < SAMP)
    def _():
        even = c == 0
        for s in range(32):
            v = []
            for x in range(2):
                at = s * 16 + 8 * x
                mine, other = got_ref[at : at + 8, :], got2_ref[at : at + 8, :]
                v += [jnp.where(even, mine, other), jnp.where(even, other, mine)]
            for i in range(4):
                acc = v[i]
                for t in range(4):
                    if t != i:
                        acc = jnp.where(lane // 32 == t, pltpu.roll(v[t], (32 * (t - i)) % 128, 1), acc)
                at = s * 24 + 8 * i if i < 3 else 768 + s * 8
                z[at : at + 8, :] = acc

        near[...] = jnp.full((16, 128), -1, jnp.int32)
        for k in range(3):
            near[4 * k : 4 * k + 4, :96] = table_ref[k]
        near[12:13, :96] = ids_ref[...] % 16
        lane1 = lanes_of((1, 128))
        used = lane1 < 96

        def line(k, e):
            return near[4 * k + e : 4 * k + e + 1, :]

        none = jnp.full((1, 128), -1, jnp.int32)
        pos = [jnp.where(used, line(0, e) * 8 + line(1, e), -1) for e in range(4)]
        own = [jnp.where(used, lane1 * 8 + 4 + e, -1) for e in range(4)]
        near[13:15, :] = jnp.full((2, 128), -1, jnp.int32)

        @pl.when(first)
        def _():
            sub = lax.broadcasted_iota(jnp.int32, (128, 128), 0)
            for n, edge in enumerate((0, 2)):
                n1, e1, f1 = line(0, edge), line(1, edge), line(2, edge)
                side = 2 * (1 - (e1 >> 1)) + f1
                found = jnp.zeros((16, 128), F32)
                for e in range(4):
                    one = jnp.where((sub == n1) & (side == e), 1.0, 0.0).astype(BF16)
                    rows = jnp.concatenate([line(0, e), line(1, e), line(2, e), jnp.zeros((13, 128), jnp.int32)], axis=0)
                    rows = jnp.where(lanes_of((16, 128)) < 96, rows, 0).astype(F32).astype(BF16)
                    found = found + jnp.dot(rows, one, preferred_element_type=F32)
                found = found.astype(jnp.int32)
                n2, e2, f2 = found[0:1], found[1:2], found[2:3]
                b2 = (e1 & 1) ^ f2
                row = jnp.where(e2 < 2, e2, b2)
                col = jnp.where(e2 < 2, b2, e2 - 2)
                s2 = (n2 * 43) >> 7
                spare = 768 + s2 * 8 + 3 * col + (n2 - 3 * s2)
                near[13 + n : 14 + n, :] = jnp.where(used, jnp.where(row == 0, n2 * 8 + 6 + col, spare), -1)

        more0 = jnp.where(first, pos[2], jnp.where(last, pos[3], none))
        more1 = jnp.where(first, pos[3], jnp.where(last, pos[2], none))
        picks = [
            [own[0], pos[0], more0, near[13:14, :], near[14:15, :]],
            [own[1], pos[1], more1],
            [own[2], pos[2]],
            [own[3], pos[3]],
        ]
        sub = lax.broadcasted_iota(jnp.int32, (128, 128), 0)
        for block in range(8):
            at = sub + 128 * block
            for e in range(4):
                total = jnp.zeros((128, 128), F32)
                for p in picks[e]:
                    total = total + jnp.where(at == p, 1.0, 0.0)
                sel[128 * block : 128 * block + 128, 128 * e : 128 * e + 128] = total.astype(BF16)
        sub16 = lax.broadcasted_iota(jnp.int32, (16, 128), 0)
        mine = sub16 == near[12:13, :]
        weight = [jnp.sum(jnp.where(mine, areas[16 * e : 16 * e + 16, :], 0.0), axis=0, keepdims=True) for e in range(4)]
        turned = jnp.concatenate([jnp.transpose(z[128 * b : 128 * b + 128, :]) for b in range(8)], axis=1)
        hi, lo = halves(turned)
        both = jnp.dot(jnp.concatenate([hi, lo], axis=0), sel[...], preferred_element_type=F32)
        hi, lo = halves((both[:128] + both[128:]) * jnp.concatenate(weight, axis=1))
        full[...] += self_product(jnp.concatenate([hi, lo], axis=0))

    mine_ref[...] = full[pl.ds(pl.multiple_of(64 * xl + 32 * c, 32), 32), :]
    other_ref[...] = full[pl.ds(pl.multiple_of(64 * (1 - xl) + 32 * c, 32), 32), :]


def body(pw_field, cell_area, tile_ids, edge_table):
    table = jnp.transpose(edge_table, (0, 2, 1))
    small = jnp.asarray(np.concatenate([lane_tables(), row_edge_table(), col_edge_table()]))
    vm = pl.BlockSpec(memory_space=pltpu.VMEM)
    sm = pl.BlockSpec(memory_space=pltpu.SMEM)
    hbm = pl.BlockSpec(memory_space=pl.ANY)
    keep, send, edges, areas = pl.pallas_call(
        filter_kernel,
        in_specs=[hbm] * 9,
        out_specs=[vm] * 4,
        scratch_shapes=[
            pltpu.VMEM((3, SB, CELLS), F32),
            pltpu.VMEM((16, CELLS), F32),
            pltpu.VMEM((2, 1536, 256), BF16),
            pltpu.VMEM((1536, 256), BF16),
            pltpu.VMEM((SB, PAD + CELLS + 512), F32),
            pltpu.VMEM((2, 2, 432, 1536), BF16),
            pltpu.VMEM((2, 2, 16, 1536), F32),
            pltpu.VMEM((8, 384), F32),
            pltpu.VMEM((6, SB, 384), F32),
            pltpu.VMEM((384, 256), BF16),
            pltpu.VMEM((192, 1536), BF16),
            pltpu.VMEM((8, 128, 128), F32),
            pltpu.SMEM((96,), jnp.int32),
            pltpu.SMEM((3, 4, 96), jnp.int32),
            pltpu.VMEM((256, 128), BF16),
            pltpu.VMEM((32, 128), F32),
            pltpu.VMEM((8, 384), F32),
            pltpu.SemaphoreType.DMA((3 * PARTS,)),
            pltpu.SemaphoreType.DMA((PARTS,)),
            pltpu.SemaphoreType.DMA((7,)),
        ],
        out_shape=[
            jax.ShapeDtypeStruct((9, 32, 384), F32),
            jax.ShapeDtypeStruct((9, 32, 384), F32),
            jax.ShapeDtypeStruct((512, 128), F32),
            jax.ShapeDtypeStruct((64, 128), F32),
        ],
        compiler_params=pltpu.CompilerParams(vmem_limit_bytes=VMEM_LIMIT),
        name="filter",
    )(
        tile_ids, table, pw_field, cell_area, jnp.asarray(quad_matrices()), jnp.asarray(col_edge_matrix()),
        jnp.asarray(row_edge_matrix()), small, jnp.asarray(inner_mask()),
    )

    flip = [(0, 1), (1, 0)]
    recv = lax.ppermute(send, "xl", flip)
    keep2 = lax.ppermute(keep, "c", flip)
    got = lax.all_to_all(edges.reshape(64, 8, 128), AXES[:4], 0, 0).reshape(512, 128)
    got2 = lax.ppermute(got, "c", flip)
    recv2 = lax.ppermute(recv, "c", flip)
    inner = pl.pallas_call(
        inner_kernel,
        in_specs=[vm] * 4,
        out_specs=vm,
        scratch_shapes=[
            pltpu.VMEM((4, 9, 32, 384), F32),
            pltpu.VMEM((256, 3456), BF16),
            pltpu.SemaphoreType.DMA((4,)),
        ],
        out_shape=jax.ShapeDtypeStruct((128, 128), F32),
        compiler_params=pltpu.CompilerParams(vmem_limit_bytes=12 * 2**20),
        name="inner",
    )(keep, recv, keep2, recv2)
    mine, other = pl.pallas_call(
        edge_kernel,
        in_specs=[vm] * 6,
        out_specs=[vm] * 2,
        scratch_shapes=[
            pltpu.VMEM((1024, 128), F32),
            pltpu.VMEM((16, 128), jnp.int32),
            pltpu.VMEM((1024, 512), BF16),
            pltpu.VMEM((128, 128), F32),
            pltpu.VMEM((512, 128), F32),
            pltpu.VMEM((512, 128), F32),
            pltpu.VMEM((64, 128), F32),
            pltpu.SemaphoreType.DMA((4,)),
        ],
        out_shape=[jax.ShapeDtypeStruct((32, 128), F32)] * 2,
        compiler_params=pltpu.CompilerParams(vmem_limit_bytes=12 * 2**20),
        name="edge",
    )(tile_ids.reshape(1, 96), table, got, got2, areas, inner)
    across = lax.ppermute(other, ("xh", "xl"), [(0, 3), (1, 2), (2, 1), (3, 0)])
    line = mine + lax.ppermute(mine, "xh", flip) + lax.ppermute(other, "xl", flip) + across
    spread = jnp.broadcast_to(line[None], (16, 32, 128))
    return jnp.sum(lax.all_to_all(spread, ("y", "z"), 0, 0), axis=0) / (96 * SAMP * SAMP)


def solution(mesh):
    fine = Mesh(mesh.devices.reshape(4, 4, 2, 2, 2), AXES)
    tm = ("xl", "c")
    placed = (P(("y", "z", "xh"), tm, None), P(), P(), P())
    return jax.shard_map(body, mesh=fine, in_specs=placed, out_specs=P(tm, None), check_vma=False)
```

```python
import functools

import jax
import jax.numpy as jnp
import ml_dtypes
import numpy as np
from jax import lax
from jax.experimental import pallas as pl
from jax.experimental.pallas import tpu as pltpu
from jax.sharding import Mesh
from jax.sharding import PartitionSpec as P

STRIDE = 4
STEPS = 4
TILE = 192
CELLS = TILE * TILE
SAMP = TILE // STRIDE
AXES = ("y", "z", "xh", "xl", "c")
PAD = 640
SB = 32
PARTS = 4
PART = CELLS // PARTS
VMEM_LIMIT = 60 * 2**20
F32 = jnp.float32
BF16 = jnp.bfloat16


def stencil():
    k = np.zeros((9, 9))
    k[4, 4] = 1.0
    for step in range(STEPS):
        c = 0.12 + 0.1 * step / max(STEPS - 1, 1)
        p = np.pad(k, 1)
        lap = p[:-2, 1:-1] + p[2:, 1:-1] + p[1:-1, :-2] + p[1:-1, 2:] - 4 * k
        k = k + c * lap
    return k[4:, 4:]


K = stencil()


def coef(d, m):
    return float(K[d, m]) if d + m <= STEPS else 0.0


CORNER = coef(2, 2) / 2.0
NEAR = {1: 0, 0: 1, 2: 1, 3: 2}
FAR = {1: 4, 0: 3, 2: 3, 3: 9}


def lane_tables():
    lane = np.arange(128) % 4
    near = np.array([[coef(d, NEAR[l]) for l in lane] for d in range(5)])
    far = np.array([[coef(d, FAR[l]) for l in lane] for d in range(2)])
    return np.concatenate([near, far, np.zeros((1, 128))]).astype(np.float32)


def edge_coef(high, flip, depth, pos):
    m = NEAR[(pos % 4) if not flip else ((3 - pos) % 4)]
    return coef(depth + 2 + high, m)


def row_edge_table():
    out = np.zeros((16, 128))
    for high in range(2):
        for flip in range(2):
            for depth in range(3):
                for lane in range(128):
                    out[(2 * high + flip) * 4 + depth, lane] = edge_coef(high, flip, depth, lane)
    return out.astype(np.float32)


def col_lanes():
    where = {}
    for k in range(8):
        for par in range(2):
            for depth in range(3):
                where[((0 if par == 0 else 64) + depth + 6 * k) % 128] = (2 * k + par, 2, depth)
                where[((63 if par == 0 else 127) - depth + 6 * k) % 128] = (2 * k + par, 3, depth)
    return where


def col_edge_table():
    out = np.zeros((8, 128))
    for lane, (row, edge, depth) in col_lanes().items():
        for high in range(2):
            for flip in range(2):
                out[(edge - 2) * 4 + 2 * high + flip, lane] = edge_coef(high, flip, depth, row)
    return out.astype(np.float32)


def place(lanes, pos, j, value=1.0):
    lanes[pos, j] = value


def sum_matrix():
    s = np.zeros((384, SAMP))
    for c in range(TILE):
        for j in range(SAMP):
            d = abs(c - (4 * j + 1))
            if 3 <= d <= 4:
                s[c, j] = 1.0
            if d <= 2:
                s[192 + c, j] = 1.0
    return s


def quad_matrices():
    s = sum_matrix()
    a = np.zeros((4, 384, 256))
    b = np.zeros((4, 384, 256))
    for q in range(4):
        a[q, :, 48 * q : 48 * q + 48] = s
        a[q, :, 192 + q] = s[:, 0]
        a[q, :, 196 + q] = s[:, SAMP - 1]
        b[q, :, 64 + 48 * q : 64 + 48 * q + 48] = s
        b[q, :, q] = s[:, 0]
        b[q, :, 4 + q] = s[:, SAMP - 1]
    both = np.stack([a.reshape(1536, 256), b.reshape(1536, 256)])
    return both.astype(ml_dtypes.bfloat16)


def row_edge_matrix():
    m = np.zeros((256, 128))
    for pos in range(TILE):
        for j in range(SAMP):
            if abs(pos - (4 * j + 1)) <= 2:
                m[pos, j] = 1.0
            if abs((TILE - 1 - pos) - (4 * j + 1)) <= 2:
                m[pos, 64 + j] = 1.0
    for k in range(2):
        m[192 + k, 48 + k] = 1.0
        m[192 + k, 112 + k] = 1.0
    return m.astype(ml_dtypes.bfloat16)


def col_edge_matrix():
    m = np.zeros((12, 128, 256))
    for group in range(12):
        for lane, (row, edge, _) in col_lanes().items():
            pos = 16 * group + row
            for j in range(SAMP):
                if abs(pos - (4 * j + 1)) <= 2:
                    m[group, lane, (edge - 2) * 128 + j] = 1.0
                if abs((TILE - 1 - pos) - (4 * j + 1)) <= 2:
                    m[group, lane, (edge - 2) * 128 + 64 + j] = 1.0
    return m.reshape(1536, 256).astype(ml_dtypes.bfloat16)


def inner_mask():
    m = np.zeros((8, 384))
    for g in range(6):
        for lane in range(384):
            r, j = 8 * g + lane // 48, lane % 48
            m[g, lane] = float(0 < r < SAMP - 1 and 0 < j < SAMP - 1)
    return m.astype(np.float32)


def halves(v):
    hi = v.astype(BF16)
    return hi, (v - hi.astype(F32)).astype(BF16)


def lanes_of(shape):
    return lax.broadcasted_iota(jnp.int32, shape, len(shape) - 1)


def space_index():
    return lax.axis_index("y") * 8 + lax.axis_index("z") * 2 + lax.axis_index("xh")


def swap_ends(v, lane):
    return jnp.where(
        lane == 0,
        pltpu.roll(v, 128 - (SAMP - 1), 1),
        jnp.where(lane == SAMP - 1, pltpu.roll(v, SAMP - 1, 1), v),
    )


def filter_kernel(
    ids_hbm, table_hbm, x_hbm, area_hbm, quad_hbm, colm_hbm, rowm_hbm, small_hbm, mask_hbm,
    keep_ref, send_ref, edge_ref, areas_ref,
    xs, area, quads, colm, wp, lhs, stage, root, packed, lrow, lcol, strip, ids, table, rowm_ref, small_ref, mask_ref,
    sem_x, sem_a, sem_c, sem_o,
):
    xl = lax.axis_index("xl")
    lane = lanes_of((SB, 128))
    first_slot = 3 * space_index()

    def copy_x(tile, part):
        at = pl.ds(part * PART, PART)
        return pltpu.make_async_copy(x_hbm.at[tile, :, at], xs.at[tile, :, at], sem_x.at[tile * PARTS + part])

    def copy_area(part):
        at = pl.ds(part * PART, PART)
        return pltpu.make_async_copy(area_hbm.at[:, at], area.at[:, at], sem_a.at[part])

    copy_quads = pltpu.make_async_copy(quad_hbm, quads, sem_c.at[0])
    copy_colm = pltpu.make_async_copy(colm_hbm, colm, sem_c.at[1])
    early = [
        pltpu.make_async_copy(src, dst, sem_c.at[2 + n])
        for n, (src, dst) in enumerate(((ids_hbm, ids), (table_hbm, table), (small_hbm, small_ref)))
    ]
    late = [
        pltpu.make_async_copy(src, dst, sem_c.at[5 + n])
        for n, (src, dst) in enumerate(((rowm_hbm, rowm_ref), (mask_hbm, mask_ref)))
    ]
    for copy in early:
        copy.start()
    for part in range(2):
        copy_area(part).start()
        copy_x(0, part).start()
    for copy in late:
        copy.start()
    wp[:, :PAD] = jnp.zeros((SB, PAD), F32)
    wp[:, PAD + CELLS :] = jnp.zeros((SB, 512), F32)
    strip[:, 96:, :] = jnp.zeros((8, 32, 128), F32)
    stage[...] = jnp.zeros((2, 2, 16, 1536), F32)
    wide = lambda k: jnp.concatenate([k, k], axis=1)
    for copy in early + late:
        copy.wait()
    near = [wide(small_ref[d : d + 1, :]) for d in range(5)]
    far = [wide(small_ref[5 + d : 6 + d, :]) for d in range(2)]
    lane2 = lanes_of((SB, 256))
    lane_one = lanes_of((1, 256))
    picked = (lane_one >= 64) & (lane_one % 4 == 1)

    def win(off):
        return wp[:, PAD + off : PAD + off + 256]

    def give(tile):
        to = pl.ds(3 * tile, 3)
        return [
            pltpu.make_async_copy(packed.at[tile, pl.ds(3 * side, 3)], ref.at[to], sem_o.at[2 * tile + n])
            for n, (side, ref) in enumerate(((xl, keep_ref), (1 - xl, send_ref)))
        ]

    def collect(tile):
        if tile == 0:
            copy_quads.wait()
        outs, area_outs = [], []
        for n in range(2):
            v = stage[tile % 2, n]
            hi = v.astype(BF16)
            rest = v - hi.astype(F32)
            mid = rest.astype(BF16)
            lhs[tile % 2, n, 384:400, :] = hi
            lhs[tile % 2, n, 400:416, :] = mid
            lhs[tile % 2, n, 416:432, :] = (rest - mid.astype(F32)).astype(BF16)
            o = jnp.dot(lhs[tile % 2, n], quads[n], preferred_element_type=F32)
            outs.append(o[:192] + o[192:384])
            area_outs.append(o[384:392] + o[400:408] + o[416:424])
        out_a, out_b = outs
        a, b = area_outs
        lane8 = lanes_of((8, 128))
        mean = jnp.concatenate([a[:, :128], jnp.where(lane8 < 64, a[:, 128:], b[:, :128]), b[:, 128:]], axis=1)
        inner = mask_ref[...] > 0.0
        root[...] = jnp.where(inner, lax.rsqrt(jnp.where(inner, mean, 1.0)), 0.0)

        left = jnp.zeros((SB, 128), F32)
        right = jnp.zeros((SB, 128), F32)
        for g in range(6):
            a, b = out_a[SB * g : SB * g + SB], out_b[SB * g : SB * g + SB]
            a1, b0 = a[:, 128:], b[:, :128]
            packed[tile, g, :, 0:128] = a[:, :128] * root[g : g + 1, 0:128]
            packed[tile, g, :, 128:256] = jnp.where(lane < 64, a1, b0) * root[g : g + 1, 128:256]
            packed[tile, g, :, 256:384] = b[:, 128:] * root[g : g + 1, 256:384]
            at_a = (lane >= 8 * g) & (lane < 8 * g + 4)
            at_b = (lane >= 8 * g + 4) & (lane < 8 * g + 8)
            left = jnp.where(at_a, pltpu.roll(a1, (8 * g + 64) % 128, 1), left)
            left = jnp.where(at_b, pltpu.roll(b0, (8 * g + 4) % 128, 1), left)
            right = jnp.where(at_a, pltpu.roll(a1, (8 * g + 60) % 128, 1), right)
            right = jnp.where(at_b, b0 if g == 0 else pltpu.roll(b0, 8 * g, 1), right)
        for copy in give(tile):
            copy.start()
        here = slice(32 * tile, 32 * tile + 32)
        strip[4, here, :] = out_a[:SB, :128]
        strip[5, here, :] = swap_ends(pltpu.roll(out_b[160:192, 128:], 48, 1), lane)
        strip[6, here, :] = left
        strip[7, here, :] = swap_ends(right, lane)


    for tile in range(3):
        slot = first_slot + tile
        aid = ids[slot] % 16
        area8 = pl.multiple_of((aid // 8) * 8, 8)
        turn = (8 - aid % 8) % 8
        row0 = tile * 32

        def area_row(off, size):
            return pltpu.roll(area[pl.ds(area8, 8), off : off + size], turn, 0)[0:1]

        def variant(edge):
            return (table[1, edge, slot] & 1) * 2 + table[2, edge, slot]

        k2 = small_ref[pl.ds(24 + variant(2), 1), :] + small_ref[pl.ds(28 + variant(3), 1), :]

        for q in range(PARTS):
            if tile == 0:
                copy_area(q).wait()
            copy_x(tile, q).wait()
            if tile == 0 and q + 2 < PARTS:
                copy_area(q + 2).start()
                copy_x(0, q + 2).start()
            if q == 1 and tile == 0:
                copy_quads.start()
            if q == 1 and tile < 2:
                for n in range(PARTS):
                    copy_x(tile + 1, n).start()
            if q == 1 and tile == 1:
                copy_colm.start()
            for g in range(3 * q, 3 * q + 3):
                acc = None
                for k in range(8):
                    vs = []
                    for part in range(3):
                        off = g * 3072 + (3 * k + part) * 128
                        w = xs[tile, :, off : off + 128] * area_row(off, 128)
                        wp[:, PAD + off : PAD + off + 128] = w
                        vs.append(w)
                    both = jnp.where(lane < 3, vs[0], jnp.where(lane >= 125, vs[2], vs[1]))
                    if k == 0:
                        acc = both
                    else:
                        moved = pltpu.roll(both, 6 * k, 1)
                        mine = ((lane >= 6 * k - 3) & (lane < 6 * k + 3)) | ((lane >= 61 + 6 * k) & (lane < 67 + 6 * k))
                        acc = jnp.where(mine, moved, acc)
                hi, lo = halves(acc * k2)
                lcol[row0 : row0 + SB, g * 128 : g * 128 + 128] = hi
                lcol[96 + row0 : 96 + row0 + SB, g * 128 : g * 128 + 128] = lo

            if q == 1 and tile > 0:
                collect(tile - 1)
            for r in range(max(0, 12 * q - 1), 12 * q + 11 if q < PARTS - 1 else SAMP):
                g, h = r // 8, r % 8
                base = 768 * r
                s0 = win(base + 128)
                s1 = win(base + 384) + win(base)
                s2 = win(base + 512) + win(base - 256)
                s3 = win(base + 768) + win(base - 384)
                s4 = win(base + 896) + win(base - 640)
                va = near[0] * s0 + near[2] * s2 + near[4] * s4
                vb = near[1] * s1 + near[3] * s3
                v1 = va + pltpu.roll(vb, 64, 1)
                v2 = far[1] * s1 + pltpu.roll(far[0] * s0, 192, 1)
                parts = [v2[:, :128], jnp.where(lane < 64, v2[:, 128:], v1[:, :128]), v1[:, 128:]]
                for p, v in enumerate(parts):
                    hi, lo = halves(v)
                    at = (h % 4) * 384 + p * 128
                    lhs[tile % 2, h // 4, g * SB : g * SB + SB, at : at + 128] = hi
                    lhs[tile % 2, h // 4, 192 + g * SB : 192 + g * SB + SB, at : at + 128] = lo
                at = (h % 4) * 384 + 128
                stage[tile % 2, h // 4, g : g + 1, at : at + 256] = jnp.where(picked, area_row(base + 128, 256), 0.0)

        for edge in range(2):
            if edge == 0:
                lines = [win(0), pltpu.roll(win(128), 192, 1), win(384)]
            else:
                lines = [pltpu.roll(win(36608), 192, 1), win(36480), pltpu.roll(win(36224), 192, 1)]
            v = variant(edge) * 4
            u = jnp.zeros((SB, 256), F32)
            for d in range(3):
                u = u + wide(small_ref[pl.ds(8 + v + d, 1), :]) * lines[d]
            first, second = lines[0][:, :128], lines[0][:, 128:]
            u1 = jnp.where(
                lane == 64,
                pltpu.roll(first, 64, 1) * CORNER,
                jnp.where(lane == 65, pltpu.roll(second, 2, 1) * CORNER, u[:, 128:]),
            )
            for p, v in enumerate((u[:, :128], u1)):
                hi, lo = halves(v)
                at = edge * 96 + row0
                lrow[at : at + SB, 128 * p : 128 * p + 128] = hi
                lrow[192 + at : 192 + at + SB, 128 * p : 128 * p + 128] = lo

    collect(2)
    copy_colm.wait()
    cr = jnp.dot(lrow[...], rowm_ref[...], preferred_element_type=F32)
    cc = jnp.dot(lcol[...], colm[...], preferred_element_type=F32)
    cr = cr[:192] + cr[192:]
    cc = cc[:96] + cc[96:]
    given = [cr[:96], cr[96:], cc[:, :128], cc[:, 128:]]
    for edge in range(4):
        for t in range(3):
            slot = first_slot + t
            v = given[edge][32 * t : 32 * t + 32]
            v = jnp.where(table[2, edge, slot] == 1, pltpu.roll(v, 64, 1), v)
            strip[edge, 32 * t : 32 * t + 32, :] = jnp.where(table[1, edge, slot] & 1 == 1, swap_ends(v, lane), v)
    turned = []
    for q in range(8):
        tr = jnp.transpose(strip[q])
        edge_ref[pl.ds(q, SAMP, stride=8), :] = tr[:SAMP]
        if q < 2:
            turned.append([tr[48:49], tr[49:50]])
    lane1 = lanes_of((1, 128))
    edge_ref[6:7, :] = turned[0][0]
    edge_ref[7:8, :] = turned[0][1]
    for end in range(2):
        for t in range(3):
            at = 3 * end + t
            moved = pltpu.roll(turned[1][end], 96 - 32 * t, 1)
            edge_ref[at : at + 1, :] = jnp.where(lane1 >= 96, moved, edge_ref[at : at + 1, :])

    chip = space_index() * 2 + xl
    ends = (chip == 0) | (chip == SAMP - 1)
    place = jnp.minimum(chip, SAMP - 1)
    cell = 4 * place + 1
    swap = 4 * jnp.where(ends, SAMP - 1 - place, place) + 1
    lane16 = lanes_of((16, 128))
    for e, spot in enumerate((192 + cell, 189 * 192 + swap, cell * 192 + 1, cell * 192 + 189)):
        a = area[:, pl.ds(pl.multiple_of((spot // 128) * 128, 128), 128)]
        a = jnp.sum(jnp.where(lane16 == spot % 128, a, 0.0), axis=1, keepdims=True)
        v = jnp.broadcast_to(lax.rsqrt(a), (16, 128))
        if e >= 2:
            v = jnp.where(ends, 0.0, v)
        areas_ref[16 * e : 16 * e + 16, :] = v
    for tile in range(3):
        for copy in give(tile):
            copy.wait()


def inner_kernel(keep_ref, recv_ref, keep2_ref, recv2_ref, out_ref, buf, hl, sem):
    xl, c = lax.axis_index("xl"), lax.axis_index("c")
    copies = [
        pltpu.make_async_copy(ref, buf.at[n], sem.at[n])
        for n, ref in enumerate((keep_ref, recv_ref, keep2_ref, recv2_ref))
    ]
    for copy in copies:
        copy.start()
    for n, row in enumerate((2 * xl + c, 2 * (1 - xl) + c, 2 * xl + 1 - c, 2 * (1 - xl) + 1 - c)):
        copies[n].wait()
        at = pl.multiple_of(row * 32, 32)
        for b in range(9):
            hi, lo = halves(buf[n, b])
            hl[pl.ds(at, 32), 384 * b : 384 * b + 384] = hi
            hl[pl.ds(pl.multiple_of(128 + at, 32), 32), 384 * b : 384 * b + 384] = lo
    out_ref[...] = self_product(hl[...])


def self_product(hl):
    g = lax.dot_general(hl[:128], hl, (((1,), (1,)), ((), ())), preferred_element_type=F32)
    cross = g[:, 128:]
    return g[:, :128] + cross + jnp.transpose(cross)


def edge_kernel(
    ids_ref, table_ref, got_hbm, got2_hbm, areas_hbm, inner_hbm, mine_ref, other_ref,
    z, near, sel, full, got_ref, got2_ref, areas, sem,
):
    copies = [
        pltpu.make_async_copy(src, dst, sem.at[n])
        for n, (src, dst) in enumerate(((got_hbm, got_ref), (got2_hbm, got2_ref), (areas_hbm, areas), (inner_hbm, full)))
    ]
    for copy in copies:
        copy.start()
    xl, c = lax.axis_index("xl"), lax.axis_index("c")
    chip = space_index() * 2 + xl
    first, last = chip == 0, chip == SAMP - 1
    lane = lanes_of((8, 128))
    for copy in copies:
        copy.wait()

    @pl.when(chip < SAMP)
    def _():
        even = c == 0
        for s in range(32):
            v = []
            for x in range(2):
                at = s * 16 + 8 * x
                mine, other = got_ref[at : at + 8, :], got2_ref[at : at + 8, :]
                v += [jnp.where(even, mine, other), jnp.where(even, other, mine)]
            for i in range(4):
                acc = v[i]
                for t in range(4):
                    if t != i:
                        acc = jnp.where(lane // 32 == t, pltpu.roll(v[t], (32 * (t - i)) % 128, 1), acc)
                at = s * 24 + 8 * i if i < 3 else 768 + s * 8
                z[at : at + 8, :] = acc

        near[...] = jnp.full((16, 128), -1, jnp.int32)
        for k in range(3):
            near[4 * k : 4 * k + 4, :96] = table_ref[k]
        near[12:13, :96] = ids_ref[...] % 16
        lane1 = lanes_of((1, 128))
        used = lane1 < 96

        def line(k, e):
            return near[4 * k + e : 4 * k + e + 1, :]

        none = jnp.full((1, 128), -1, jnp.int32)
        pos = [jnp.where(used, line(0, e) * 8 + line(1, e), -1) for e in range(4)]
        own = [jnp.where(used, lane1 * 8 + 4 + e, -1) for e in range(4)]
        near[13:15, :] = jnp.full((2, 128), -1, jnp.int32)

        @pl.when(first)
        def _():
            sub = lax.broadcasted_iota(jnp.int32, (128, 128), 0)
            for n, edge in enumerate((0, 2)):
                n1, e1, f1 = line(0, edge), line(1, edge), line(2, edge)
                side = 2 * (1 - (e1 >> 1)) + f1
                found = jnp.zeros((16, 128), F32)
                for e in range(4):
                    one = jnp.where((sub == n1) & (side == e), 1.0, 0.0).astype(BF16)
                    rows = jnp.concatenate([line(0, e), line(1, e), line(2, e), jnp.zeros((13, 128), jnp.int32)], axis=0)
                    rows = jnp.where(lanes_of((16, 128)) < 96, rows, 0).astype(F32).astype(BF16)
                    found = found + jnp.dot(rows, one, preferred_element_type=F32)
                found = found.astype(jnp.int32)
                n2, e2, f2 = found[0:1], found[1:2], found[2:3]
                b2 = (e1 & 1) ^ f2
                row = jnp.where(e2 < 2, e2, b2)
                col = jnp.where(e2 < 2, b2, e2 - 2)
                s2 = (n2 * 43) >> 7
                spare = 768 + s2 * 8 + 3 * col + (n2 - 3 * s2)
                near[13 + n : 14 + n, :] = jnp.where(used, jnp.where(row == 0, n2 * 8 + 6 + col, spare), -1)

        more0 = jnp.where(first, pos[2], jnp.where(last, pos[3], none))
        more1 = jnp.where(first, pos[3], jnp.where(last, pos[2], none))
        picks = [
            [own[0], pos[0], more0, near[13:14, :], near[14:15, :]],
            [own[1], pos[1], more1],
            [own[2], pos[2]],
            [own[3], pos[3]],
        ]
        sub = lax.broadcasted_iota(jnp.int32, (128, 128), 0)
        for block in range(8):
            at = sub + 128 * block
            for e in range(4):
                total = jnp.zeros((128, 128), F32)
                for p in picks[e]:
                    total = total + jnp.where(at == p, 1.0, 0.0)
                sel[128 * block : 128 * block + 128, 128 * e : 128 * e + 128] = total.astype(BF16)
        sub16 = lax.broadcasted_iota(jnp.int32, (16, 128), 0)
        mine = sub16 == near[12:13, :]
        weight = [jnp.sum(jnp.where(mine, areas[16 * e : 16 * e + 16, :], 0.0), axis=0, keepdims=True) for e in range(4)]
        turned = jnp.concatenate([jnp.transpose(z[128 * b : 128 * b + 128, :]) for b in range(8)], axis=1)
        hi, lo = halves(turned)
        both = jnp.dot(jnp.concatenate([hi, lo], axis=0), sel[...], preferred_element_type=F32)
        hi, lo = halves((both[:128] + both[128:]) * jnp.concatenate(weight, axis=1))
        full[...] += self_product(jnp.concatenate([hi, lo], axis=0))

    mine_ref[...] = full[pl.ds(pl.multiple_of(64 * xl + 32 * c, 32), 32), :]
    other_ref[...] = full[pl.ds(pl.multiple_of(64 * (1 - xl) + 32 * c, 32), 32), :]


def body(pw_field, cell_area, tile_ids, edge_table):
    table = jnp.transpose(edge_table, (0, 2, 1))
    small = jnp.asarray(np.concatenate([lane_tables(), row_edge_table(), col_edge_table()]))
    vm = pl.BlockSpec(memory_space=pltpu.VMEM)
    sm = pl.BlockSpec(memory_space=pltpu.SMEM)
    hbm = pl.BlockSpec(memory_space=pl.ANY)
    keep, send, edges, areas = pl.pallas_call(
        filter_kernel,
        in_specs=[hbm] * 9,
        out_specs=[hbm, hbm, vm, vm],
        scratch_shapes=[
            pltpu.VMEM((3, SB, CELLS), F32),
            pltpu.VMEM((16, CELLS), F32),
            pltpu.VMEM((2, 1536, 256), BF16),
            pltpu.VMEM((1536, 256), BF16),
            pltpu.VMEM((SB, PAD + CELLS + 512), F32),
            pltpu.VMEM((2, 2, 432, 1536), BF16),
            pltpu.VMEM((2, 2, 16, 1536), F32),
            pltpu.VMEM((8, 384), F32),
            pltpu.VMEM((3, 6, SB, 384), F32),
            pltpu.VMEM((384, 256), BF16),
            pltpu.VMEM((192, 1536), BF16),
            pltpu.VMEM((8, 128, 128), F32),
            pltpu.SMEM((96,), jnp.int32),
            pltpu.SMEM((3, 4, 96), jnp.int32),
            pltpu.VMEM((256, 128), BF16),
            pltpu.VMEM((32, 128), F32),
            pltpu.VMEM((8, 384), F32),
            pltpu.SemaphoreType.DMA((3 * PARTS,)),
            pltpu.SemaphoreType.DMA((PARTS,)),
            pltpu.SemaphoreType.DMA((7,)),
            pltpu.SemaphoreType.DMA((6,)),
        ],
        out_shape=[
            jax.ShapeDtypeStruct((9, 32, 384), F32),
            jax.ShapeDtypeStruct((9, 32, 384), F32),
            jax.ShapeDtypeStruct((512, 128), F32),
            jax.ShapeDtypeStruct((64, 128), F32),
        ],
        compiler_params=pltpu.CompilerParams(vmem_limit_bytes=VMEM_LIMIT),
        name="filter",
    )(
        tile_ids, table, pw_field, cell_area, jnp.asarray(quad_matrices()), jnp.asarray(col_edge_matrix()),
        jnp.asarray(row_edge_matrix()), small, jnp.asarray(inner_mask()),
    )

    flip = [(0, 1), (1, 0)]
    recv = lax.ppermute(send, "xl", flip)
    keep2 = lax.ppermute(keep, "c", flip)
    got = lax.all_to_all(edges.reshape(64, 8, 128), AXES[:4], 0, 0).reshape(512, 128)
    got2 = lax.ppermute(got, "c", flip)
    recv2 = lax.ppermute(recv, "c", flip)
    inner = pl.pallas_call(
        inner_kernel,
        in_specs=[vm] * 4,
        out_specs=vm,
        scratch_shapes=[
            pltpu.VMEM((4, 9, 32, 384), F32),
            pltpu.VMEM((256, 3456), BF16),
            pltpu.SemaphoreType.DMA((4,)),
        ],
        out_shape=jax.ShapeDtypeStruct((128, 128), F32),
        compiler_params=pltpu.CompilerParams(vmem_limit_bytes=12 * 2**20),
        name="inner",
    )(keep, recv, keep2, recv2)
    mine, other = pl.pallas_call(
        edge_kernel,
        in_specs=[vm] * 6,
        out_specs=[vm] * 2,
        scratch_shapes=[
            pltpu.VMEM((1024, 128), F32),
            pltpu.VMEM((16, 128), jnp.int32),
            pltpu.VMEM((1024, 512), BF16),
            pltpu.VMEM((128, 128), F32),
            pltpu.VMEM((512, 128), F32),
            pltpu.VMEM((512, 128), F32),
            pltpu.VMEM((64, 128), F32),
            pltpu.SemaphoreType.DMA((4,)),
        ],
        out_shape=[jax.ShapeDtypeStruct((32, 128), F32)] * 2,
        compiler_params=pltpu.CompilerParams(vmem_limit_bytes=12 * 2**20),
        name="edge",
    )(tile_ids.reshape(1, 96), table, got, got2, areas, inner)
    across = lax.ppermute(other, ("xh", "xl"), [(0, 3), (1, 2), (2, 1), (3, 0)])
    line = mine + lax.ppermute(mine, "xh", flip) + lax.ppermute(other, "xl", flip) + across
    spread = jnp.broadcast_to(line[None], (16, 32, 128))
    return jnp.sum(lax.all_to_all(spread, ("y", "z"), 0, 0), axis=0) / (96 * SAMP * SAMP)


def solution(mesh):
    fine = Mesh(mesh.devices.reshape(4, 4, 2, 2, 2), AXES)
    tm = ("xl", "c")
    placed = (P(("y", "z", "xh"), tm, None), P(), P(), P())
    return jax.shard_map(body, mesh=fine, in_specs=placed, out_specs=P(tm, None), check_vma=False)
```
